256 devices in a mesh: chol: 32 (over x, z_hi, y), walk: 8 (over z_lo, core).
Axes of the slice: x: 4, y: 4, z: 8 (z_hi: 2, z_lo: 4; z = z_hi * 4 + z_lo), core: 2. Of those that a mesh axis runs over, the one named last changes fastest.
Arguments:
- green: bfloat16 [32, 120, 320], P('walk'), may hold values from -6 to 6
- walkers: bfloat16 [32, 320, 120], P('walk', 'chol'), may hold values from -6 to 6
- chol_rot: bfloat16 [3840, 120, 320], P(('chol', 'walk')), may hold values from -0.0625 to 0.0625
- chol_full: bfloat16 [3840, 320, 320], P(('chol', 'walk')), may hold values from -0.0625 to 0.0625
- fields: float32 [3840, 32], P(('chol', 'walk')), may hold values from -6 to 6
- one_body_rot: bfloat16 [120, 320], replicated, may hold values from -0.03125 to 0.03125
Outputs:
- new_walkers: bfloat16 [32, 320, 120], P('walk', 'chol')
- energy: float32 [32], replicated
- log_weight: float32 [32], replicated
The draws below stay inside these ranges and needn't reach their ends.
All inputs are finite; a program needn't handle non-finite values.
Results may differ from the reference program's by a relative error of at most 0.024.
Values may be sent and summed in bfloat16 or wider, within the bound.
No kernel may reach another device: no remote copies, remote signals or barrier semaphores. Data moves between devices by JAX's collectives and lax.ppermute only.
A program may use at most 192 MiB of HBM per device.

```python
import jax
import jax.numpy as jnp
from jax import lax

N = 320
NE = 120
NCHOL = 3840
ORDER = 4
W = 32


def levels(own_key, dims, cuts, least, top_value):
    gain, own = 1.0, jax.random.fold_in(own_key, 6)
    for position, blocks in cuts:
        heights = jnp.exp(jax.random.uniform(jax.random.fold_in(own, position), (blocks,), jnp.float32, least / len(cuts), top_value / len(cuts)))
        gain = gain * jnp.repeat(heights, dims[position] // blocks).reshape([-1 if axis == position else 1 for axis in range(len(dims))])
    return gain


def bell_draw(stream_key, shape, deviation, reach, pieces=(), dtype=jnp.bfloat16):
    level = levels(stream_key, shape, pieces, -0.22, 0.18) if pieces else 1.0
    drawn = jax.random.normal(stream_key, shape, jnp.float32) * deviation * level
    return jnp.minimum(jnp.maximum(drawn, -reach), reach).astype(dtype)


def setup_inputs(seed: int = 0) -> dict:
    keys = jax.random.split(jax.random.key(seed), 7)
    return {
        "green": bell_draw(keys[0], (W, NE, N), 1.0, 6.0, ((0, 8),)),
        "walkers": bell_draw(keys[1], (W, N, NE), 1.0, 6.0, ((0, 8), (1, 32))),
        "chol_rot": bell_draw(keys[2], (NCHOL, NE, N), (NE * N // 4) ** -0.5, 0.0625, ((0, 256),)),
        "chol_full": bell_draw(keys[3], (NCHOL, N, N), (N * NCHOL // 144) ** -0.5, 0.0625, ((0, 256),)),
        "fields": bell_draw(keys[4], (NCHOL, W), 1.0, 6.0, ((0, 256),), jnp.float32),
        "one_body_rot": bell_draw(keys[5], (NE, N), (NE * N) ** -0.5, 0.03125),
    }


step_root = 0.1


def reference(green, walkers, chol_rot, chol_full, fields, one_body_rot):
    walker_count = green.shape[0]
    flat_green = green.reshape(walker_count, NE * N)
    intersection = jnp.dot(chol_rot.reshape(NCHOL, NE * N), flat_green.T, preferred_element_type=jnp.float32)
    bias = 2.0 * step_root * intersection
    log_weight = jnp.sum(fields * bias - 0.5 * bias * bias, axis=0) / (NCHOL ** 0.5)
    single = 2.0 * jnp.dot(flat_green, one_body_rot.reshape(NE * N), preferred_element_type=jnp.float32)
    block_size = 16
    blocks = chol_rot.reshape(NCHOL // block_size, block_size, NE, N)
    green_wide = green.astype(jnp.float32)

    def exchange_block(total, block):
        pairs = jnp.einsum('gin,wjn->gwij', block.astype(jnp.float32), green_wide)
        return total - jnp.einsum('gwij,gwji->w', pairs, pairs), None

    exchange_total, unused = lax.scan(exchange_block, jnp.zeros((walker_count,), jnp.float32), blocks)
    energy = single + (jnp.sum(2.0 * intersection * intersection, axis=0) + exchange_total) / NCHOL
    shifted = (fields - bias).astype(jnp.bfloat16)
    field = jnp.dot(shifted.T, chol_full.reshape(NCHOL, N * N), preferred_element_type=jnp.float32)
    field = (step_root * field).astype(jnp.bfloat16).reshape(walker_count, N, N).astype(jnp.float32)
    current = walkers
    accumulated = walkers.astype(jnp.float32)
    for order in range(1, ORDER + 1):
        update = jnp.einsum('wpq,wqe->wpe', field, current.astype(jnp.float32)) / order
        accumulated = accumulated + update
        current = update.astype(jnp.bfloat16)
    return accumulated.astype(jnp.bfloat16), energy, log_weight
```

```python
import functools

import jax
import jax.numpy as jnp
from jax import lax
from jax.experimental import pallas as pl
from jax.experimental.pallas import tpu as pltpu
from jax.sharding import Mesh, PartitionSpec as P

ORDER = 4
step_root = 0.1

AXES = ("x", "zh", "y", "zl", "core")
SIZES = (4, 2, 4, 4, 2)
Z = ("zh", "zl")
HIGH = ("x", "zh", "y")
LOW = ("zl", "core")

ROW = 128
WIDE = 384
TILE = 16
f32 = jnp.float32
bf16 = jnp.bfloat16
CONTRACT_LAST = (((1,), (1,)), ((), ()))


def ring(count, shift):
    return [(i, (i + shift) % count) for i in range(count)]


def parts_of(value):
    high = value.astype(bf16).astype(f32)
    rest = value - high
    middle = rest.astype(bf16).astype(f32)
    low = (rest - middle).astype(bf16).astype(f32)
    row = lax.broadcasted_iota(jnp.int32, (TILE, value.shape[1]), 0)
    zero = jnp.zeros((TILE, value.shape[1]), f32)
    return jnp.where(
        row == 0, high, jnp.where(row == 1, middle, jnp.where(row == 2, low, zero))
    )


def pair_kernel(vectors, *refs):
    rot_ref, greens, (trace_ref, square_ref) = refs[0], refs[1:-2], refs[-2:]
    orbitals = rot_ref.shape[2]
    eye = (
        lax.broadcasted_iota(jnp.int32, (ROW, ROW), 0)
        == lax.broadcasted_iota(jnp.int32, (ROW, ROW), 1)
    ).astype(f32)
    base = 0
    for green_ref in greens:
        count = green_ref.shape[0] // 2

        def two_walkers(i, carry, green_ref=green_ref, base=base):
            green = green_ref[pl.ds(2 * i, 2)].reshape(2 * ROW, orbitals)
            rot = rot_ref[...].reshape(vectors * ROW, orbitals)
            pairs = lax.dot_general(rot, green, CONTRACT_LAST, preferred_element_type=f32)
            for w in range(2):
                total = jnp.zeros((8, ROW), f32)
                for g in range(vectors):
                    block = pairs[g * ROW : (g + 1) * ROW, w * ROW : (w + 1) * ROW]
                    total = total + jnp.sum((block * block.T).reshape(ROW // 8, 8, ROW), axis=0)
                    trace_ref[base + 2 * i + w, pl.ds(g, 1), :] = jnp.sum(
                        block * eye, axis=0, keepdims=True
                    )
                square_ref[base + 2 * i + w] = total
            return carry

        if count == 1:
            two_walkers(0, 0)
        else:
            lax.fori_loop(0, count, two_walkers, 0)
        base += 2 * count


def pair_sums(rot, greens):
    vectors = rot.shape[0]
    walkers = sum(g.shape[0] for g in greens)
    return pl.pallas_call(
        functools.partial(pair_kernel, vectors),
        out_shape=(
            jax.ShapeDtypeStruct((walkers, vectors, ROW), f32),
            jax.ShapeDtypeStruct((walkers, 8, ROW), f32),
        ),
        compiler_params=pltpu.CompilerParams(vmem_limit_bytes=40 * 2**20),
        cost_estimate=pl.CostEstimate(
            flops=4 * walkers * vectors * ROW * ROW * 512, bytes_accessed=3 * 2**20, transcendentals=0
        ),
        name="pairs",
    )(rot, *greens)


def field_kernel(vectors, order_ref, message_ref, *refs):
    blocks, out_ref = refs[:-1], refs[-1]
    rows, orbitals = blocks[0].shape[1:]
    depth = vectors * TILE
    spread = (
        lax.broadcasted_iota(jnp.int32, (ROW, depth), 0)
        == lax.shift_right_logical(lax.broadcasted_iota(jnp.int32, (ROW, depth), 1), 4)
    ).astype(bf16)
    same = (
        jnp.bitwise_and(lax.broadcasted_iota(jnp.int32, (TILE * TILE, depth), 0), TILE - 1)
        == jnp.bitwise_and(lax.broadcasted_iota(jnp.int32, (TILE * TILE, depth), 1), TILE - 1)
    )
    weights = []
    for b in range(len(blocks)):
        shifted = message_ref[order_ref[b], 0:TILE, :].astype(bf16)
        wide = jnp.dot(shifted, spread, preferred_element_type=f32)
        wide = jnp.broadcast_to(wide[:, None, :], (TILE, TILE, depth)).reshape(TILE * TILE, depth)
        weights.append(jnp.where(same, wide, 0.0).astype(bf16))
    out_ref[:, :, :, 256:WIDE] = jnp.zeros((4, 4, rows, WIDE - 256), bf16)
    for t in range(rows // TILE):
        total = jnp.zeros((TILE * TILE, orbitals), f32)
        for b, block_ref in enumerate(blocks):
            block = block_ref[:, t * TILE : (t + 1) * TILE, :].reshape(depth, orbitals)
            total = total + jnp.dot(weights[b], block, preferred_element_type=f32)
        total = (step_root * total).astype(bf16).reshape(TILE, TILE, orbitals)
        for w in range(TILE):
            out_ref[w % 4, w // 4, t * TILE : (t + 1) * TILE, 0:orbitals] = total[w]
    scalars = message_ref[0, TILE : TILE + 1, :]
    for s in range(1, len(blocks)):
        scalars = scalars + message_ref[s, TILE : TILE + 1, :]
    scalars = parts_of(scalars).astype(bf16)
    upper = lax.broadcasted_iota(jnp.int32, (TILE, 128), 1) >= 64
    for w in range(4):
        held = out_ref[w, 0, 0:TILE, 256:WIDE]
        out_ref[w, 0, 0:TILE, 256:WIDE] = jnp.where(upper, scalars, held)


def field_rows(order, message, blocks):
    vectors, rows, orbitals = blocks[0].shape
    return pl.pallas_call(
        functools.partial(field_kernel, vectors),
        out_shape=jax.ShapeDtypeStruct((4, 4, rows, WIDE), bf16),
        in_specs=[pl.BlockSpec(memory_space=pltpu.SMEM)]
        + [pl.BlockSpec(memory_space=pltpu.VMEM)] * (1 + len(blocks)),
        compiler_params=pltpu.CompilerParams(vmem_limit_bytes=40 * 2**20),
        cost_estimate=pl.CostEstimate(
            flops=2 * 256 * 256 * 384 * 40, bytes_accessed=5 * 2**20, transcendentals=0
        ),
        name="field_rows",
    )(order, message, *blocks)


def sum_kernel(copies, in_ref, out_ref):
    upper = lax.broadcasted_iota(jnp.int32, (TILE, 128), 1) >= 64
    sources, groups = in_ref.shape[:2]
    for g in range(groups):
        total = in_ref[0, g].astype(f32)
        for s in range(1, sources):
            total = total + in_ref[s, g].astype(f32)
        if g == 0:
            first = total[0:TILE, 256:WIDE]
            scalars = parts_of(jnp.sum(first, axis=0, keepdims=True))
        rounded = total.astype(bf16)
        corner = jnp.where(upper, scalars, total[0:TILE, 256:WIDE]).astype(bf16)
        for k in range(g, copies, groups):
            out_ref[k] = rounded
            out_ref[k, 0:TILE, 256:WIDE] = corner


def sum_over_y(received):
    _, _, rows, wide = received.shape
    return pl.pallas_call(
        functools.partial(sum_kernel, 8),
        out_shape=jax.ShapeDtypeStruct((8, rows, wide), bf16),
        compiler_params=pltpu.CompilerParams(vmem_limit_bytes=24 * 2**20),
        name="sum_y",
    )(received)


def last_kernel(in_ref, walker_ref, out_ref, scalars_ref):
    total = in_ref[0].astype(f32)
    for s in range(1, in_ref.shape[0]):
        total = total + in_ref[s].astype(f32)
    rounded = total.astype(bf16)
    scalars_ref[...] = jnp.sum(total[0:TILE, 256:WIDE], axis=0, keepdims=True)
    for k in range(4):
        out_ref[k, :, 0:WIDE] = rounded
        out_ref[k, :, WIDE : WIDE + 128] = walker_ref[...]


def sum_over_z(received, walker_rows):
    _, rows, wide = received.shape
    return pl.pallas_call(
        last_kernel,
        out_shape=(
            jax.ShapeDtypeStruct((4, rows, wide + 128), bf16),
            jax.ShapeDtypeStruct((1, 128), f32),
        ),
        compiler_params=pltpu.CompilerParams(vmem_limit_bytes=24 * 2**20),
        name="sum_z",
    )(received, walker_rows)


def taylor_kernel(orbitals, in_ref, out_ref):
    whole = in_ref[...].reshape(orbitals, in_ref.shape[2])
    field = whole[:, 0:orbitals]
    current = whole[:, WIDE : WIDE + 128]
    total = current.astype(f32)
    for order in range(1, ORDER + 1):
        update = jnp.dot(field, current, preferred_element_type=f32) / order
        total = total + update
        current = update.astype(bf16)
    out_ref[...] = total.astype(bf16)


def taylor(gathered):
    orbitals = gathered.shape[0] * gathered.shape[1]
    return pl.pallas_call(
        functools.partial(taylor_kernel, orbitals),
        out_shape=jax.ShapeDtypeStruct((orbitals, 128), bf16),
        compiler_params=pltpu.CompilerParams(vmem_limit_bytes=24 * 2**20),
        name="taylor",
    )(gathered)


def by_source(relative, index):
    turned = jnp.concatenate([relative[0:1], relative[3:4], relative[2:3], relative[1:2]])
    twice = jnp.concatenate([turned, turned])
    return lax.dynamic_slice_in_dim(twice, lax.rem(4 - index, 4), 4, axis=0)


def on_device(green, walkers, chol_rot, chol_full, fields, one_body_rot):
    x, zh, y, zl, core = (lax.axis_index(a) for a in AXES)
    vectors, electrons, orbitals = chol_rot.shape
    vector_total = vectors * 256
    rows = orbitals // 4
    group = green.shape[0]

    def swap(a):
        return lax.ppermute(a, "core", ring(2, 1))

    padded = jnp.pad(green, ((0, 0), (0, ROW - electrons), (0, 0)))
    rot = jnp.pad(chol_rot, ((0, 0), (0, ROW - electrons), (0, 0)))
    before = lax.ppermute(padded, Z, ring(8, 1))
    after = lax.ppermute(padded, Z, ring(8, -1))
    far_a = lax.ppermute(padded[:2], Z, ring(8, 2))
    far_b = lax.ppermute(padded[2:], Z, ring(8, -2))

    def rows_of(position):
        return lax.dynamic_slice_in_dim(chol_full, lax.rem(position, 4) * rows, rows, axis=1)

    mine = [rows_of(x)]
    for k in (1, 2, 3):
        mine.append(lax.ppermute(rows_of(x + k), "x", ring(4, k)))
    blocks, order = [], []
    for k in range(4):
        source = 2 * lax.rem(x + 4 - k, 4)
        blocks += [mine[k], swap(mine[k])]
        order += [source + core, source + 1 - core]

    held = [lax.dynamic_slice_in_dim(walkers, y, 1, axis=0)]
    for k in (1, 2, 3):
        piece = lax.dynamic_slice_in_dim(walkers, lax.rem(y + k, 4), 1, axis=0)
        held.append(lax.ppermute(piece, "y", ring(4, k)))
    held = by_source(jnp.concatenate(held), y).reshape(rows // 2, electrons)
    other = lax.ppermute(held, "zh", ring(2, 1))
    walker_rows = jnp.where(
        zh == 0, jnp.concatenate([held, other]), jnp.concatenate([other, held])
    )
    walker_rows = jnp.pad(walker_rows, ((0, 0), (0, 128 - electrons)))

    shards = [
        [padded, swap(padded)],
        [before, swap(before)],
        [far_a, far_b, swap(far_a), swap(far_b)],
        [after, swap(after)],
    ]
    sums = [pair_sums(rot, shards[d]) for d in (0, 1, 3, 2)]
    sums = [sums[0], sums[1], sums[3], sums[2]]
    traces = jnp.stack([jnp.sum(s[0], axis=-1) for s in sums]).reshape(4, 2, group, vectors)
    squares = jnp.stack([jnp.sum(s[1], axis=(1, 2)) for s in sums]).reshape(4, 2, group)
    single = 2.0 * jnp.sum(green.astype(f32) * one_body_rot.astype(f32), axis=(1, 2))
    squares = squares.at[0, 0].add(single * (-vector_total / 32.0))

    def by_group(a):
        a = jnp.where(core == 0, a, a[:, ::-1])
        return by_source(a, zl)

    intersection = by_group(traces).reshape(8 * group, vectors)
    exchange = by_group(squares).reshape(8 * group)
    bias = 2.0 * step_root * intersection
    noise = fields.T
    weight_part = jnp.sum(noise * bias - 0.5 * bias * bias, axis=1) / vector_total**0.5
    energy_part = (
        jnp.sum(2.0 * intersection * intersection, axis=1) - exchange
    ) / vector_total
    shifted = (noise - bias).astype(bf16).astype(f32)
    shifted = shifted.reshape(4, 2, group, vectors).transpose(1, 0, 2, 3).reshape(2, 4 * group, vectors)
    scalars = jnp.concatenate([energy_part, weight_part])
    message = jnp.concatenate(
        [
            jnp.pad(shifted, ((0, 0), (0, 0), (0, 128 - vectors))),
            jnp.broadcast_to(jnp.pad(scalars, (64, 0))[None, None], (2, 1, 128)),
            jnp.zeros((2, 7, 128), f32),
        ],
        axis=1,
    )
    message = jnp.broadcast_to(message[None], (4, 2, 24, 128)).reshape(8, 24, 128)
    message = lax.all_to_all(message, ("x", "core"), 0, 0)

    field = field_rows(jnp.stack(order).astype(jnp.int32), message, blocks)
    field = lax.all_to_all(field, "y", 0, 0)
    field = sum_over_y(field)
    field = lax.all_to_all(field, Z, 0, 0)
    field, scalars = sum_over_z(field, walker_rows)
    field = lax.all_to_all(field, "x", 0, 0)
    whole = taylor(field)[:, :electrons]
    new = lax.dynamic_slice_in_dim(whole, rows * x + (rows // 2) * zh, rows // 2, axis=0)
    new = lax.all_to_all(new.reshape(4, rows // 8, electrons), "y", 0, 0)
    return new, scalars[0, 64:96], scalars[0, 96:128]


def solution(mesh):
    split = Mesh(mesh.devices.reshape(SIZES), AXES)
    in_specs = (
        P(LOW, None, None),
        P(LOW, HIGH, None),
        P(HIGH + LOW, None, None),
        P(HIGH + LOW, None, None),
        P(HIGH + LOW, None),
        P(),
    )
    out_specs = (P(LOW, HIGH, None), P(), P())
    return jax.shard_map(
        on_device, mesh=split, in_specs=in_specs, out_specs=out_specs, check_vma=False
    )
```

```python
import functools

import jax
import jax.numpy as jnp
from jax import lax
from jax.experimental import pallas as pl
from jax.experimental.pallas import tpu as pltpu
from jax.sharding import Mesh, PartitionSpec as P

ORDER = 4
step_root = 0.1

AXES = ("x", "zh", "y", "zl", "core")
SIZES = (4, 2, 4, 4, 2)
Z = ("zh", "zl")
HIGH = ("x", "zh", "y")
LOW = ("zl", "core")

ROW = 128
WIDE = 384
TILE = 16
f32 = jnp.float32
bf16 = jnp.bfloat16
CONTRACT_LAST = (((1,), (1,)), ((), ()))


def ring(count, shift):
    return [(i, (i + shift) % count) for i in range(count)]


def parts_of(value):
    high = value.astype(bf16).astype(f32)
    rest = value - high
    middle = rest.astype(bf16).astype(f32)
    low = (rest - middle).astype(bf16).astype(f32)
    row = lax.broadcasted_iota(jnp.int32, (TILE, value.shape[1]), 0)
    zero = jnp.zeros((TILE, value.shape[1]), f32)
    return jnp.where(
        row == 0, high, jnp.where(row == 1, middle, jnp.where(row == 2, low, zero))
    )


def pair_kernel(vectors, turned, walkers, *refs):
    rot_ref, greens = refs[0], refs[1 : 1 + walkers]
    trace_ref, square_ref = refs[1 + walkers : 3 + walkers]
    if not turned:
        raw_ref, rot_ref = rot_ref, refs[3 + walkers]
        for g in range(vectors):
            rot_ref[g] = widen(raw_ref[g]).T
    orbitals = rot_ref.shape[2]
    eye = (
        lax.broadcasted_iota(jnp.int32, (ROW, ROW), 0)
        == lax.broadcasted_iota(jnp.int32, (ROW, ROW), 1)
    ).astype(f32)
    base = 0
    for green_ref in greens:
        count = green_ref.shape[0] // 2

        def two_walkers(i, carry, green_ref=green_ref, base=base):
            green = jnp.concatenate([widen(green_ref[2 * i]), widen(green_ref[2 * i + 1])], axis=1)
            rot = rot_ref[...].reshape(vectors * ROW, orbitals)
            pairs = jnp.dot(rot, green, preferred_element_type=f32)
            for w in range(2):
                total = jnp.zeros((8, ROW), f32)
                for g in range(vectors):
                    block = pairs[g * ROW : (g + 1) * ROW, w * ROW : (w + 1) * ROW]
                    total = total + jnp.sum((block * block.T).reshape(ROW // 8, 8, ROW), axis=0)
                    trace_ref[base + 2 * i + w, pl.ds(g, 1), :] = jnp.sum(
                        block * eye, axis=0, keepdims=True
                    )
                square_ref[base + 2 * i + w] = total
            return carry

        if count == 1:
            two_walkers(0, 0)
        else:
            lax.fori_loop(0, count, two_walkers, 0)
        base += 2 * count


def widen(a):
    return jnp.concatenate([a, jnp.zeros((a.shape[0], ROW - a.shape[1]), a.dtype)], axis=1)


def pair_sums(rot, greens, turned):
    vectors = rot.shape[0]
    walkers = sum(g.shape[0] for g in greens)
    out_shape = [
        jax.ShapeDtypeStruct((walkers, vectors, ROW), f32),
        jax.ShapeDtypeStruct((walkers, 8, ROW), f32),
    ]
    if not turned:
        out_shape.append(jax.ShapeDtypeStruct((vectors, ROW, rot.shape[1]), bf16))
    return pl.pallas_call(
        functools.partial(pair_kernel, vectors, turned, len(greens)),
        out_shape=out_shape,
        compiler_params=pltpu.CompilerParams(vmem_limit_bytes=40 * 2**20),
        cost_estimate=pl.CostEstimate(
            flops=4 * walkers * vectors * ROW * ROW * 512, bytes_accessed=3 * 2**20, transcendentals=0
        ),
        name="pairs",
    )(rot, *greens)


def field_kernel(vectors, carries, order_ref, message_ref, *refs):
    blocks, out_ref = refs[:-1], refs[-1]
    rows, orbitals = blocks[0].shape[1:]
    depth = vectors * TILE
    spread = (
        lax.broadcasted_iota(jnp.int32, (ROW, depth), 0)
        == lax.shift_right_logical(lax.broadcasted_iota(jnp.int32, (ROW, depth), 1), 4)
    ).astype(bf16)
    same = (
        jnp.bitwise_and(lax.broadcasted_iota(jnp.int32, (TILE * TILE, depth), 0), TILE - 1)
        == jnp.bitwise_and(lax.broadcasted_iota(jnp.int32, (TILE * TILE, depth), 1), TILE - 1)
    )
    weights = []
    for b in range(len(blocks)):
        shifted = message_ref[order_ref[b], 0:TILE, :].astype(bf16)
        wide = jnp.dot(shifted, spread, preferred_element_type=f32)
        wide = jnp.broadcast_to(wide[:, None, :], (TILE, TILE, depth)).reshape(TILE * TILE, depth)
        weights.append(jnp.where(same, wide, 0.0).astype(bf16))
    out_ref[:, :, :, 256:WIDE] = jnp.zeros((4, 4, rows, WIDE - 256), bf16)
    for t in range(rows // TILE):
        total = jnp.zeros((TILE * TILE, orbitals), f32)
        for b, block_ref in enumerate(blocks):
            block = block_ref[:, t * TILE : (t + 1) * TILE, :].reshape(depth, orbitals)
            total = total + jnp.dot(weights[b], block, preferred_element_type=f32)
        total = (step_root * total).astype(bf16).reshape(TILE, TILE, orbitals)
        for w in range(TILE):
            out_ref[w % 4, w // 4, t * TILE : (t + 1) * TILE, 0:orbitals] = total[w]
    if not carries:
        return
    scalars = message_ref[0, TILE : TILE + 1, :]
    for s in range(1, len(blocks)):
        scalars = scalars + message_ref[s, TILE : TILE + 1, :]
    scalars = parts_of(scalars).astype(bf16)
    upper = lax.broadcasted_iota(jnp.int32, (TILE, 128), 1) >= 64
    for w in range(4):
        held = out_ref[w, 0, 0:TILE, 256:WIDE]
        out_ref[w, 0, 0:TILE, 256:WIDE] = jnp.where(upper, scalars, held)


def field_rows(order, message, blocks, carries):
    vectors, rows, orbitals = blocks[0].shape
    return pl.pallas_call(
        functools.partial(field_kernel, vectors, carries),
        out_shape=jax.ShapeDtypeStruct((4, 4, rows, WIDE), bf16),
        in_specs=[pl.BlockSpec(memory_space=pltpu.SMEM)]
        + [pl.BlockSpec(memory_space=pltpu.VMEM)] * (1 + len(blocks)),
        compiler_params=pltpu.CompilerParams(vmem_limit_bytes=40 * 2**20),
        cost_estimate=pl.CostEstimate(
            flops=rows * 256 * 384 * 256, bytes_accessed=rows * 60000, transcendentals=0
        ),
        name="field_rows",
    )(order, message, *blocks)


def sum_kernel(copies, first_ref, second_ref, out_ref):
    upper = lax.broadcasted_iota(jnp.int32, (TILE, 128), 1) >= 64
    sources, groups, rows = first_ref.shape[:3]
    for g in range(groups):
        total = first_ref[0, g].astype(f32)
        below = second_ref[0, g].astype(f32)
        for s in range(1, sources):
            total = total + first_ref[s, g].astype(f32)
            below = below + second_ref[s, g].astype(f32)
        if g == 0:
            scalars = parts_of(jnp.sum(total[0:TILE, 256:WIDE], axis=0, keepdims=True))
        corner = jnp.where(upper, scalars, total[0:TILE, 256:WIDE]).astype(bf16)
        total, below = total.astype(bf16), below.astype(bf16)
        for k in range(g, copies, groups):
            out_ref[k, 0:rows] = total
            out_ref[k, rows:] = below
            out_ref[k, 0:TILE, 256:WIDE] = corner


def sum_second_axis(first, second):
    rows, wide = first.shape[2] + second.shape[2], first.shape[3]
    return pl.pallas_call(
        functools.partial(sum_kernel, 8),
        out_shape=jax.ShapeDtypeStruct((8, rows, wide), bf16),
        compiler_params=pltpu.CompilerParams(vmem_limit_bytes=24 * 2**20),
        name="sum_plane",
    )(first, second)


def last_kernel(in_ref, out_ref, scalars_ref):
    total = in_ref[0].astype(f32)
    for s in range(1, in_ref.shape[0]):
        total = total + in_ref[s].astype(f32)
    rounded = total.astype(bf16)
    scalars_ref[...] = jnp.sum(total[0:TILE, 256:WIDE], axis=0, keepdims=True)
    for k in range(out_ref.shape[0]):
        out_ref[k] = rounded


def sum_over_z(received):
    _, rows, wide = received.shape
    return pl.pallas_call(
        last_kernel,
        out_shape=(
            jax.ShapeDtypeStruct((16, rows, wide), bf16),
            jax.ShapeDtypeStruct((1, 128), f32),
        ),
        compiler_params=pltpu.CompilerParams(vmem_limit_bytes=24 * 2**20),
        name="sum_z",
    )(received)


def taylor_kernel(first_rows, in_ref, walkers_ref, out_ref):
    orbitals = walkers_ref.shape[1]
    for w in range(4):
        field = jnp.concatenate(
            [in_ref[4 * k + w, 0:first_rows] for k in range(4)]
            + [in_ref[4 * w + k, first_rows:] for k in range(4)]
        )[:, 0:orbitals]
        current = walkers_ref[w]
        total = current.astype(f32)
        for order in range(1, ORDER + 1):
            update = jnp.dot(field, current, preferred_element_type=f32) / order
            total = total + update
            current = update.astype(bf16)
        out_ref[w] = total.astype(bf16)


def taylor(gathered, walkers, first_rows):
    return pl.pallas_call(
        functools.partial(taylor_kernel, first_rows),
        out_shape=jax.ShapeDtypeStruct(walkers.shape, bf16),
        compiler_params=pltpu.CompilerParams(vmem_limit_bytes=24 * 2**20),
        name="taylor",
    )(gathered, walkers)


def by_source(relative, index):
    turned = jnp.concatenate([relative[0:1], relative[3:4], relative[2:3], relative[1:2]])
    twice = jnp.concatenate([turned, turned])
    return lax.dynamic_slice_in_dim(twice, lax.rem(4 - index, 4), 4, axis=0)


def on_device(green, walkers, chol_rot, chol_full, fields, one_body_rot):
    x, zh, y, zl, core = (lax.axis_index(a) for a in AXES)
    vectors, electrons, orbitals = chol_rot.shape
    vector_total = vectors * 256
    group = green.shape[0]
    tiles = orbitals // TILE
    first_rows = TILE * ((tiles // 4 + 1) // 2)
    second_rows = orbitals // 4 - first_rows

    def swap(a):
        return lax.ppermute(a, "core", ring(2, 1))

    turned = green.swapaxes(1, 2)
    before = lax.ppermute(turned, Z, ring(8, 1))
    after = lax.ppermute(turned, Z, ring(8, -1))
    far_a = lax.ppermute(turned[:2], Z, ring(8, 2))
    far_b = lax.ppermute(turned[2:], Z, ring(8, -2))

    def rows_of_vectors(axis, position, start, rows):
        def rows_of(k):
            first = start + lax.rem(position + k, 4) * rows
            return lax.dynamic_slice_in_dim(chol_full, first, rows, axis=1)

        mine = [rows_of(0)]
        for k in (1, 2, 3):
            mine.append(lax.ppermute(rows_of(k), axis, ring(4, k)))
        blocks, order = [], []
        for k in range(4):
            source = 2 * lax.rem(position + 4 - k, 4)
            blocks += [mine[k], swap(mine[k])]
            order += [source + core, source + 1 - core]
        return blocks, jnp.stack(order).astype(jnp.int32)

    first_blocks, first_order = rows_of_vectors("x", x, 0, first_rows)
    second_blocks, second_order = rows_of_vectors("y", y, 4 * first_rows, second_rows)

    whole = jnp.broadcast_to(walkers[None], (32,) + walkers.shape)
    whole = lax.all_to_all(whole, HIGH, 0, 0)
    whole = whole.transpose(1, 0, 2, 3).reshape(group, orbitals, electrons)

    shards = [
        [turned, swap(turned)],
        [before, swap(before)],
        [far_a, far_b, swap(far_a), swap(far_b)],
        [after, swap(after)],
    ]
    own = pair_sums(chol_rot.swapaxes(1, 2), shards[0], False)
    sums = [own] + [pair_sums(own[2], shards[d], True) for d in (1, 2, 3)]
    traces = jnp.stack([jnp.sum(s[0], axis=-1) for s in sums]).reshape(4, 2, group, vectors)
    squares = jnp.stack([jnp.sum(s[1], axis=(1, 2)) for s in sums]).reshape(4, 2, group)
    single = 2.0 * jnp.sum(green.astype(f32) * one_body_rot.astype(f32), axis=(1, 2))
    squares = squares.at[0, 0].add(single * (-vector_total / 32.0))

    def by_group(a):
        a = jnp.where(core == 0, a, a[:, ::-1])
        return by_source(a, zl)

    intersection = by_group(traces).reshape(8 * group, vectors)
    exchange = by_group(squares).reshape(8 * group)
    bias = 2.0 * step_root * intersection
    noise = fields.T
    weight_part = jnp.sum(noise * bias - 0.5 * bias * bias, axis=1) / vector_total**0.5
    energy_part = (
        jnp.sum(2.0 * intersection * intersection, axis=1) - exchange
    ) / vector_total
    shifted = (noise - bias).astype(bf16).astype(f32)
    shifted = shifted.reshape(4, 2, group, vectors).transpose(1, 0, 2, 3).reshape(2, 4 * group, vectors)
    scalars = jnp.concatenate([energy_part, weight_part])
    message = jnp.concatenate(
        [
            jnp.pad(shifted, ((0, 0), (0, 0), (0, 128 - vectors))),
            jnp.broadcast_to(jnp.pad(scalars, (64, 0))[None, None], (2, 1, 128)),
            jnp.zeros((2, 7, 128), f32),
        ],
        axis=1,
    )
    message = jnp.broadcast_to(message[None], (4, 2, 24, 128)).reshape(8, 24, 128)
    first = lax.all_to_all(message, ("x", "core"), 0, 0)
    second = lax.all_to_all(message, ("y", "core"), 0, 0)

    first = field_rows(first_order, first, first_blocks, True)
    first = lax.all_to_all(first, "y", 0, 0)
    second = field_rows(second_order, second, second_blocks, False)
    second = lax.all_to_all(second, "x", 0, 0)
    field = sum_second_axis(first, second)
    field = lax.all_to_all(field, Z, 0, 0)
    field, scalars = sum_over_z(field)
    field = lax.all_to_all(field, ("x", "y"), 0, 0)
    new = taylor(field, whole, first_rows)
    share = orbitals // 32
    new = lax.dynamic_slice_in_dim(new, share * (8 * x + 4 * zh + y), share, axis=1)
    return new, scalars[0, 64:96], scalars[0, 96:128]


def solution(mesh):
    split = Mesh(mesh.devices.reshape(SIZES), AXES)
    in_specs = (
        P(LOW, None, None),
        P(LOW, HIGH, None),
        P(HIGH + LOW, None, None),
        P(HIGH + LOW, None, None),
        P(HIGH + LOW, None),
        P(),
    )
    out_specs = (P(LOW, HIGH, None), P(), P())
    return jax.shard_map(
        on_device, mesh=split, in_specs=in_specs, out_specs=out_specs, check_vma=False
    )
```

```python
import functools

import jax
import jax.numpy as jnp
from jax import lax
from jax.experimental import pallas as pl
from jax.experimental.pallas import tpu as pltpu
from jax.sharding import Mesh, PartitionSpec as P

ORDER = 4
step_root = 0.1

AXES = ("x", "zh", "y", "zl", "core")
SIZES = (4, 2, 4, 4, 2)
Z = ("zh", "zl")
HIGH = ("x", "zh", "y")
LOW = ("zl", "core")

ROW = 128
WIDE = 384
TILE = 16
f32 = jnp.float32
bf16 = jnp.bfloat16
CONTRACT_LAST = (((1,), (1,)), ((), ()))


def after(value, *others):
    return lax.optimization_barrier((value, *others))[0]


def ring(count, shift):
    return [(i, (i + shift) % count) for i in range(count)]


def parts_of(value):
    high = value.astype(bf16).astype(f32)
    rest = value - high
    middle = rest.astype(bf16).astype(f32)
    low = (rest - middle).astype(bf16).astype(f32)
    row = lax.broadcasted_iota(jnp.int32, (TILE, value.shape[1]), 0)
    zero = jnp.zeros((TILE, value.shape[1]), f32)
    return jnp.where(
        row == 0, high, jnp.where(row == 1, middle, jnp.where(row == 2, low, zero))
    )


def pair_kernel(vectors, turned, walkers, *refs):
    rot_ref, greens = refs[0], refs[1 : 1 + walkers]
    trace_ref, square_ref = refs[1 + walkers : 3 + walkers]
    if not turned:
        raw_ref, rot_ref = rot_ref, refs[3 + walkers]
        for g in range(vectors):
            rot_ref[g] = widen(raw_ref[g]).T
    orbitals = rot_ref.shape[2]
    eye = (
        lax.broadcasted_iota(jnp.int32, (ROW, ROW), 0)
        == lax.broadcasted_iota(jnp.int32, (ROW, ROW), 1)
    ).astype(f32)
    base = 0
    for green_ref in greens:
        count = green_ref.shape[0] // 2

        def two_walkers(i, carry, green_ref=green_ref, base=base):
            green = jnp.concatenate([widen(green_ref[2 * i]), widen(green_ref[2 * i + 1])], axis=1)
            rot = rot_ref[...].reshape(vectors * ROW, orbitals)
            pairs = jnp.dot(rot, green, preferred_element_type=f32)
            for w in range(2):
                total = jnp.zeros((8, ROW), f32)
                for g in range(vectors):
                    block = pairs[g * ROW : (g + 1) * ROW, w * ROW : (w + 1) * ROW]
                    total = total + jnp.sum((block * block.T).reshape(ROW // 8, 8, ROW), axis=0)
                    trace_ref[base + 2 * i + w, pl.ds(g, 1), :] = jnp.sum(
                        block * eye, axis=0, keepdims=True
                    )
                square_ref[base + 2 * i + w] = total
            return carry

        if count == 1:
            two_walkers(0, 0)
        else:
            lax.fori_loop(0, count, two_walkers, 0)
        base += 2 * count


def widen(a):
    return jnp.concatenate([a, jnp.zeros((a.shape[0], ROW - a.shape[1]), a.dtype)], axis=1)


def pair_sums(rot, greens, turned):
    vectors = rot.shape[0]
    walkers = sum(g.shape[0] for g in greens)
    out_shape = [
        jax.ShapeDtypeStruct((walkers, vectors, ROW), f32),
        jax.ShapeDtypeStruct((walkers, 8, ROW), f32),
    ]
    if not turned:
        out_shape.append(jax.ShapeDtypeStruct((vectors, ROW, rot.shape[1]), bf16))
    return pl.pallas_call(
        functools.partial(pair_kernel, vectors, turned, len(greens)),
        out_shape=out_shape,
        compiler_params=pltpu.CompilerParams(vmem_limit_bytes=40 * 2**20),
        cost_estimate=pl.CostEstimate(flops=1, bytes_accessed=1, transcendentals=0),
        name="pairs",
    )(rot, *greens)


def message_kernel(vector_total, place_ref, *refs):
    traces, squares = refs[0:4], refs[4:8]
    fields_ref, green_ref, one_body_ref, walkers_ref, out_ref = refs[8:]
    zl, core = place_ref[0], place_ref[1]
    vectors = fields_ref.shape[0]
    lanes = lax.broadcasted_iota(jnp.int32, (vectors, 128), 1)
    lane = lax.broadcasted_iota(jnp.int32, (1, 128), 1)
    intersection = jnp.zeros((vectors, 128), f32)
    exchange = jnp.zeros((1, 128), f32)
    single = jnp.zeros((1, 128), f32)
    one_body = one_body_ref[...].astype(f32)
    for d in range(4):
        for w in range(8):
            owner = core if w < 4 else 1 - core
            index = owner * 16 + (w % 4) * 4 + lax.rem(zl + 4 - d, 4)
            trace = jnp.sum(traces[d][w], axis=1, keepdims=True)
            intersection = jnp.where(lanes == index, trace, intersection)
            exchange = jnp.where(lane == index, jnp.sum(squares[d][w], keepdims=True), exchange)
            if d == 0 and w < 4:
                own = jnp.sum(green_ref[w].astype(f32) * one_body, keepdims=True)
                single = jnp.where(lane == index, own * (2.0 / 32.0), single)
    bias = 2.0 * step_root * intersection
    noise = fields_ref[...]
    weight = jnp.sum(noise * bias - 0.5 * bias * bias, axis=0, keepdims=True) / vector_total**0.5
    energy = jnp.sum(2.0 * intersection * intersection, axis=0, keepdims=True) - exchange
    energy = energy / vector_total + single
    shifted = jnp.concatenate([noise - bias, jnp.zeros((128 - vectors, 128), f32)]).T
    scalars = parts_of(pltpu.roll(energy, 64, 1) + pltpu.roll(weight, 96, 1))
    top = (shifted[0:TILE] + scalars).astype(bf16)
    low = shifted[TILE : 2 * TILE].astype(bf16)
    for k in range(out_ref.shape[0]):
        out_ref[k, 0:TILE] = top
        out_ref[k, TILE : 2 * TILE] = low
        out_ref[k, 2 * TILE :] = walkers_ref[...]


def messages(place, sums, fields, green, one_body, walkers):
    vectors = fields.shape[0]
    return pl.pallas_call(
        functools.partial(message_kernel, vectors * 256),
        out_shape=jax.ShapeDtypeStruct((16, 2 * TILE + walkers.shape[0], 128), bf16),
        in_specs=[pl.BlockSpec(memory_space=pltpu.SMEM)]
        + [pl.BlockSpec(memory_space=pltpu.VMEM)] * 12,
        compiler_params=pltpu.CompilerParams(vmem_limit_bytes=24 * 2**20),
        name="message",
    )(place, *[p[0] for p in sums], *[p[1] for p in sums], fields, green, one_body, walkers)


def field_kernel(vectors, count, adds, place_ref, message_ref, *refs):
    blocks, refs = refs[:count], refs[count:]
    if count == 1:
        blocks = [blocks[0].at[k] for k in range(4)]
    outs = refs[adds:]
    rows, orbitals = blocks[0].shape[1:]
    depth = vectors * TILE
    spread = (
        lax.broadcasted_iota(jnp.int32, (ROW, depth), 0)
        == lax.shift_right_logical(lax.broadcasted_iota(jnp.int32, (ROW, depth), 1), 4)
    ).astype(bf16)
    same = (
        jnp.bitwise_and(lax.broadcasted_iota(jnp.int32, (TILE * TILE, depth), 0), TILE - 1)
        == jnp.bitwise_and(lax.broadcasted_iota(jnp.int32, (TILE * TILE, depth), 1), TILE - 1)
    )
    start = pl.multiple_of(place_ref[4] * TILE, TILE)
    weights = []
    for b in range(len(blocks)):
        shifted = message_ref[place_ref[b], pl.ds(start, TILE), :].astype(f32)
        shifted = pltpu.roll(shifted, place_ref[5], 0).astype(bf16)
        wide = jnp.dot(shifted, spread, preferred_element_type=f32)
        wide = jnp.broadcast_to(wide[:, None, :], (TILE, TILE, depth)).reshape(TILE * TILE, depth)
        weights.append(jnp.where(same, wide, 0.0).astype(bf16))
    outs = [out.at[i] for out in outs for i in range(out.shape[0])]
    for out_ref in outs:
        out_ref[:, :, 256:WIDE] = jnp.zeros((4, rows, WIDE - 256), bf16)
    for t in range(rows // TILE):
        here = slice(t * TILE, (t + 1) * TILE)
        total = jnp.zeros((TILE * TILE, orbitals), f32)
        for b, block_ref in enumerate(blocks):
            block = block_ref[:, here, :].reshape(depth, orbitals)
            total = total + jnp.dot(weights[b], block, preferred_element_type=f32)
        total = (step_root * total).reshape(TILE, TILE, orbitals)
        for w in range(TILE):
            part = total[w]
            if adds:
                part = part + refs[0][w // 4, w % 4, here, 0:orbitals].astype(f32)
            outs[w // 4][w % 4, here, 0:orbitals] = part.astype(bf16)


def field_rows(place, message, blocks, other=None, pieces=1):
    vectors, rows, _ = blocks[0].shape[-3:]
    added = [] if other is None else [other]
    return pl.pallas_call(
        functools.partial(field_kernel, vectors, len(blocks), other is not None),
        out_shape=[jax.ShapeDtypeStruct((4 // pieces, 4, rows, WIDE), bf16)] * pieces,
        in_specs=[pl.BlockSpec(memory_space=pltpu.SMEM)]
        + [pl.BlockSpec(memory_space=pltpu.VMEM)] * (1 + len(blocks) + len(added)),
        compiler_params=pltpu.CompilerParams(vmem_limit_bytes=40 * 2**20),
        cost_estimate=pl.CostEstimate(
            flops=rows * 256 * 384 * 128, bytes_accessed=rows * 40000, transcendentals=0
        ),
        name="field_rows",
    )(place, message, *blocks, *added)


def sum_kernel(copies, message_ref, *refs):
    upper = lax.broadcasted_iota(jnp.int32, (TILE, 128), 1) >= 64
    scalars = message_ref[0, 0:TILE].astype(f32)
    for s in range(1, message_ref.shape[0]):
        scalars = scalars + message_ref[s, 0:TILE].astype(f32)
    scalars = parts_of(jnp.sum(scalars, axis=0, keepdims=True))
    out_ref = refs[-1]
    pieces = [ref.at[i] for ref in refs[:-1] for i in range(ref.shape[0])]
    firsts, seconds = pieces[:4], pieces[4:]
    groups, rows = firsts[0].shape[:2]
    for g in range(groups):
        total = firsts[0][g].astype(f32)
        below = seconds[0][g].astype(f32)
        for s in range(1, 4):
            total = total + firsts[s][g].astype(f32)
            below = below + seconds[s][g].astype(f32)
        corner = jnp.where(upper, scalars, total[0:TILE, 256:WIDE]).astype(bf16)
        total, below = total.astype(bf16), below.astype(bf16)
        for k in range(g, copies, groups):
            out_ref[k, 0:rows] = total
            out_ref[k, rows:] = below
            out_ref[k, 0:TILE, 256:WIDE] = corner


def sum_second_axis(message, first, second):
    rows, wide = first[0].shape[2] + second[0].shape[2], first[0].shape[3]
    return pl.pallas_call(
        functools.partial(sum_kernel, 8),
        out_shape=jax.ShapeDtypeStruct((8, rows, wide), bf16),
        compiler_params=pltpu.CompilerParams(vmem_limit_bytes=24 * 2**20),
        name="sum_plane",
    )(message, *first, *second)


def last_kernel(in_ref, out_ref, scalars_ref):
    total = in_ref[0].astype(f32)
    for s in range(1, in_ref.shape[0]):
        total = total + in_ref[s].astype(f32)
    rounded = total.astype(bf16)
    scalars_ref[...] = jnp.sum(total[0:TILE, 256:WIDE], axis=0, keepdims=True)
    for k in range(out_ref.shape[0]):
        out_ref[k] = rounded


def sum_over_z(received):
    _, rows, wide = received.shape
    return pl.pallas_call(
        last_kernel,
        out_shape=(
            jax.ShapeDtypeStruct((16, rows, wide), bf16),
            jax.ShapeDtypeStruct((1, 128), f32),
        ),
        compiler_params=pltpu.CompilerParams(vmem_limit_bytes=24 * 2**20),
        name="sum_z",
    )(received)


def taylor_kernel(first_rows, in_ref, walkers_ref, out_ref):
    orbitals = walkers_ref.shape[1]
    for w in range(4):
        field = jnp.concatenate(
            [in_ref[4 * k + w, 0:first_rows] for k in range(4)]
            + [in_ref[4 * w + k, first_rows:] for k in range(4)]
        )[:, 0:orbitals]
        current = walkers_ref[w]
        total = current.astype(f32)
        for order in range(1, ORDER + 1):
            update = jnp.dot(field, current, preferred_element_type=f32) / order
            total = total + update
            current = update.astype(bf16)
        out_ref[w] = total.astype(bf16)


def taylor(gathered, walkers, first_rows):
    return pl.pallas_call(
        functools.partial(taylor_kernel, first_rows),
        out_shape=jax.ShapeDtypeStruct(walkers.shape, bf16),
        compiler_params=pltpu.CompilerParams(vmem_limit_bytes=24 * 2**20),
        name="taylor",
    )(gathered, walkers)


def on_device(green, walkers, chol_rot, chol_full, fields, one_body_rot):
    x, zh, y, zl, core = (lax.axis_index(a) for a in AXES)
    vectors, electrons, orbitals = chol_rot.shape
    vector_total = vectors * 256
    group = green.shape[0]
    tiles = orbitals // TILE
    first_rows = TILE * ((tiles // 4 + 1) // 2)
    second_rows = orbitals // 4 - first_rows

    def swap(a):
        return lax.ppermute(a, "core", ring(2, 1))

    turned = green.swapaxes(1, 2)
    before = lax.ppermute(turned, Z, ring(8, 1))
    behind = lax.ppermute(turned, Z, ring(8, -1))
    opposite = [(2 * i + c, 2 * ((i + 2 - 4 * c) % 8) + c) for i in range(8) for c in range(2)]
    far = lax.ppermute(turned, Z + ("core",), opposite)

    first_pieces = [
        lax.dynamic_slice_in_dim(chol_full, lax.rem(x + k, 4) * first_rows, first_rows, axis=1)
        for k in range(4)
    ]
    first_blocks = first_pieces[:1] + [
        lax.ppermute(first_pieces[k], "x", ring(4, k)) for k in (1, 2, 3)
    ]
    second_piece = chol_full[:, 4 * first_rows :].reshape(vectors, 4, second_rows, orbitals)
    second_piece = second_piece.transpose(1, 0, 2, 3)
    second_block = lax.all_to_all(second_piece, "y", 0, 0)

    rot = after(chol_rot.swapaxes(1, 2), *first_pieces, second_piece)
    own = pair_sums(rot, [turned, swap(turned)], False)
    before, behind, far = (after(a, own[0]) for a in (before, behind, far))
    sums = [own] + [pair_sums(own[2], [a, swap(a)], True) for a in (before, far, behind)]

    noise = fields.reshape(vectors, 4, 2, group).transpose(0, 2, 3, 1).reshape(vectors, 8 * group)
    noise = jnp.pad(noise, ((0, 0), (0, 128 - 8 * group)))
    share = walkers.shape[1]
    near = walkers.transpose(1, 0, 2).reshape(share * group, electrons)
    near = jnp.pad(near, ((0, -share * group % TILE), (0, 128 - electrons)))
    message = messages(
        jnp.stack([zl, core]).astype(jnp.int32), sums, noise, turned, one_body_rot.T, near
    )
    message = after(message, *first_blocks, second_block)
    message = lax.all_to_all(message, ("x", "y"), 0, 0)

    def place(positions, half, shift):
        return jnp.stack([*positions, half, shift]).astype(jnp.int32)

    along_x = [4 * lax.rem(x + 4 - k, 4) + y for k in range(4)]
    along_y = [4 * x + k for k in range(4)]
    turn = lax.rem(16 - 4 * x, 16)
    (second,) = field_rows(place(along_y, 1 - core, turn), message, [second_block])
    second = swap(second)
    (first,) = field_rows(place(along_x, 1 - core, 0), message, first_blocks)
    first = swap(first)
    second = field_rows(place(along_y, core, turn), message, [second_block], second, 4)
    second = [second[0]] + [lax.ppermute(second[k], "x", ring(4, k)) for k in (1, 2, 3)]
    (first,) = field_rows(place(along_x, core, 0), message, first_blocks, first)
    first = lax.all_to_all(first, "y", 0, 0)
    near = after(message[:, 2 * TILE : 2 * TILE + share * group, :electrons], second[0])
    other = lax.ppermute(near, "zh", ring(2, 1))
    whole = jnp.where(zh == 0, jnp.stack([near, other], 1), jnp.stack([other, near], 1))
    whole = whole.reshape(4, 4, 2, share, group, electrons).transpose(4, 0, 2, 1, 3, 5)
    whole = whole.reshape(group, orbitals, electrons)
    field = sum_second_axis(message, [first], second)
    field = lax.all_to_all(field, Z, 0, 0)
    field, scalars = sum_over_z(field)
    scalars = scalars + swap(scalars)
    field = lax.all_to_all(field, ("x", "y"), 0, 0)
    new = taylor(field, whole, first_rows)
    new = lax.dynamic_slice_in_dim(new, share * (8 * x + 4 * zh + y), share, axis=1)

    def in_order(a):
        return a.reshape(2, group, 4).transpose(2, 0, 1).reshape(8 * group)

    return new, in_order(scalars[0, 64:96]), in_order(scalars[0, 96:128])


def solution(mesh):
    split = Mesh(mesh.devices.reshape(SIZES), AXES)
    in_specs = (
        P(LOW, None, None),
        P(LOW, HIGH, None),
        P(HIGH + LOW, None, None),
        P(HIGH + LOW, None, None),
        P(HIGH + LOW, None),
        P(),
    )
    out_specs = (P(LOW, HIGH, None), P(), P())
    return jax.shard_map(
        on_device, mesh=split, in_specs=in_specs, out_specs=out_specs, check_vma=False
    )
```

```python
import functools

import jax
import jax.numpy as jnp
from jax import lax
from jax.experimental import pallas as pl
from jax.experimental.pallas import tpu as pltpu
from jax.sharding import Mesh, PartitionSpec as P

ORDER = 4
step_root = 0.1

AXES = ("x", "zh", "y", "zl", "core")
SIZES = (4, 2, 4, 4, 2)
Z = ("zh", "zl")
HIGH = ("x", "zh", "y")
LOW = ("zl", "core")

ROW = 128
WIDE = 384
TILE = 16
f32 = jnp.float32
bf16 = jnp.bfloat16
CONTRACT_LAST = (((1,), (1,)), ((), ()))


def after(value, *others):
    return lax.optimization_barrier((value, *others))[0]


def ring(count, shift):
    return [(i, (i + shift) % count) for i in range(count)]


def parts_of(value):
    high = value.astype(bf16).astype(f32)
    rest = value - high
    middle = rest.astype(bf16).astype(f32)
    low = (rest - middle).astype(bf16).astype(f32)
    row = lax.broadcasted_iota(jnp.int32, (TILE, value.shape[1]), 0)
    zero = jnp.zeros((TILE, value.shape[1]), f32)
    return jnp.where(
        row == 0, high, jnp.where(row == 1, middle, jnp.where(row == 2, low, zero))
    )


def pair_kernel(vectors, first, count, *refs):
    inputs, (trace_ref, square_ref) = refs[:count], refs[count : count + 2]
    held, semaphores = refs[-1 - count : -1], refs[-1]
    loads = [
        pltpu.make_async_copy(src, dst, semaphores.at[i])
        for i, (src, dst) in enumerate(zip(inputs, held, strict=True))
    ]
    for load in loads:
        load.start()
    loads[0].wait()
    rot_ref, greens = held[0], held[1:]
    if first:
        rot_ref = refs[count + 2]
        for g in range(vectors):
            rot_ref[g] = widen(held[0][g]).T
    orbitals = rot_ref.shape[2]
    eye = (
        lax.broadcasted_iota(jnp.int32, (ROW, ROW), 0)
        == lax.broadcasted_iota(jnp.int32, (ROW, ROW), 1)
    ).astype(f32)
    base = 0
    for load, green_ref in zip(loads[1:], greens, strict=True):
        load.wait()
        count = green_ref.shape[0] // 2

        def two_walkers(i, carry, green_ref=green_ref, base=base):
            green = jnp.concatenate([widen(green_ref[2 * i]), widen(green_ref[2 * i + 1])], axis=1)
            rot = rot_ref[...].reshape(vectors * ROW, orbitals)
            pairs = jnp.dot(rot, green, preferred_element_type=f32)
            for w in range(2):
                total = jnp.zeros((8, ROW), f32)
                for g in range(vectors):
                    block = pairs[g * ROW : (g + 1) * ROW, w * ROW : (w + 1) * ROW]
                    total = total + jnp.sum((block * block.T).reshape(ROW // 8, 8, ROW), axis=0)
                    trace_ref[base + 2 * i + w, pl.ds(g, 1), :] = jnp.sum(
                        block * eye, axis=0, keepdims=True
                    )
                square_ref[base + 2 * i + w] = total
            return carry

        if count == 1:
            two_walkers(0, 0)
        else:
            lax.fori_loop(0, count, two_walkers, 0)
        base += 2 * count


def widen(a):
    return jnp.concatenate([a, jnp.zeros((a.shape[0], ROW - a.shape[1]), a.dtype)], axis=1)


def pair_sums(rot, greens, first):
    vectors = rot.shape[0]
    walkers = sum(g.shape[0] for g in greens)
    out_shape = [
        jax.ShapeDtypeStruct((walkers, vectors, ROW), f32),
        jax.ShapeDtypeStruct((walkers, 8, ROW), f32),
    ]
    if first:
        out_shape.append(jax.ShapeDtypeStruct((vectors, ROW, rot.shape[1]), bf16))
    return pl.pallas_call(
        functools.partial(pair_kernel, vectors, first, 1 + len(greens)),
        out_shape=out_shape,
        in_specs=[pl.BlockSpec(memory_space=pl.ANY)] * (1 + len(greens)),
        scratch_shapes=[pltpu.VMEM(a.shape, bf16) for a in (rot, *greens)]
        + [pltpu.SemaphoreType.DMA((1 + len(greens),))],
        compiler_params=pltpu.CompilerParams(vmem_limit_bytes=56 * 2**20),
        cost_estimate=pl.CostEstimate(flops=1, bytes_accessed=1, transcendentals=0),
        name="pairs",
    )(rot, *greens)


def message_kernel(vector_total, place_ref, *refs):
    fields_ref, green_ref, one_body_ref, give_ref, keep_ref = refs[4:]
    traces, squares = ([ref.at[w] for ref in refs[k : k + 2] for w in range(ref.shape[0])] for k in (0, 2))
    zl, core = place_ref[0], place_ref[1]
    vectors = fields_ref.shape[0]
    lanes = lax.broadcasted_iota(jnp.int32, (vectors, 128), 1)
    lane = lax.broadcasted_iota(jnp.int32, (1, 128), 1)
    intersection = jnp.zeros((vectors, 128), f32)
    exchange = jnp.zeros((1, 128), f32)
    single = jnp.zeros((1, 128), f32)
    one_body = one_body_ref[...].astype(f32)
    for d in range(4):
        for w in range(8):
            owner = core if w < 4 else 1 - core
            index = lax.rem(zl + 4 - d, 4) * 8 + owner * 4 + w % 4
            trace = jnp.sum(traces[8 * d + w][...], axis=1, keepdims=True)
            intersection = jnp.where(lanes == index, trace, intersection)
            exchange = jnp.where(lane == index, jnp.sum(squares[8 * d + w][...], keepdims=True), exchange)
            if d == 0 and w < 4:
                own = jnp.sum(green_ref[w].astype(f32) * one_body, keepdims=True)
                single = jnp.where(lane == index, own * (2.0 / 32.0), single)
    bias = 2.0 * step_root * intersection
    noise = jnp.concatenate([fields_ref[...], jnp.zeros((vectors, 96), f32)], axis=1)
    weight = jnp.sum(noise * bias - 0.5 * bias * bias, axis=0, keepdims=True) / vector_total**0.5
    energy = jnp.sum(2.0 * intersection * intersection, axis=0, keepdims=True) - exchange
    energy = energy / vector_total + single
    shifted = jnp.concatenate([noise - bias, jnp.zeros((128 - vectors, 128), f32)]).T.astype(bf16)
    row = lax.broadcasted_iota(jnp.int32, (TILE, 128), 0)
    column = lax.broadcasted_iota(jnp.int32, (TILE, 128), 1)

    def rows_of(owner):
        source = jnp.bitwise_and(row, 3) * 8 + owner * 4 + lax.shift_right_logical(row, 2)
        return jnp.dot((column == source).astype(bf16), shifted, preferred_element_type=f32)

    scalars = parts_of(pltpu.roll(energy, 64, 1) + pltpu.roll(weight, 96, 1))
    give_ref[...] = rows_of(1 - core).astype(bf16)
    keep_ref[...] = (rows_of(core) + scalars).astype(bf16)


def messages(place, sums, fields, green, one_body):
    vectors = fields.shape[0]
    return pl.pallas_call(
        functools.partial(message_kernel, vectors * 256),
        out_shape=[jax.ShapeDtypeStruct((TILE, 128), bf16)] * 2,
        in_specs=[pl.BlockSpec(memory_space=pltpu.SMEM)]
        + [pl.BlockSpec(memory_space=pltpu.VMEM)] * 7,
        compiler_params=pltpu.CompilerParams(vmem_limit_bytes=56 * 2**20),
        name="message",
    )(place, *[p[0] for p in sums], *[p[1] for p in sums], fields, green, one_body)


def copies_kernel(place_ref, keep_ref, got_ref, near_ref, other_ref, out_ref):
    rows = near_ref.shape[0]
    near = pl.ds(pl.multiple_of(TILE + rows * place_ref[0], TILE), rows)
    other = pl.ds(pl.multiple_of(TILE + rows * (1 - place_ref[0]), TILE), rows)
    got = pltpu.roll(got_ref[...].astype(f32), TILE, 1)
    top = (keep_ref[...].astype(f32) + got).astype(bf16)
    for k in range(out_ref.shape[0]):
        out_ref[k, 0:TILE] = top
        out_ref[k, near] = near_ref[...]
        out_ref[k, other] = other_ref[...]


def copies(place, keep, got, near, other):
    return pl.pallas_call(
        copies_kernel,
        out_shape=jax.ShapeDtypeStruct((16, TILE + 2 * near.shape[0], 128), bf16),
        in_specs=[pl.BlockSpec(memory_space=pltpu.SMEM)]
        + [pl.BlockSpec(memory_space=pltpu.VMEM)] * 4,
        compiler_params=pltpu.CompilerParams(vmem_limit_bytes=16 * 2**20),
        name="copies",
    )(place, keep, got, near, other)


def field_kernel(vectors, place_ref, message_ref, *refs):
    inputs = [ref for ref in refs if len(ref.shape) == 3 or ref.shape[1] == vectors]
    outs = [out.at[i] for out in refs[len(inputs) :] for i in range(out.shape[0])]
    blocks = []
    for ref in inputs:
        blocks += [ref] if len(ref.shape) == 3 else [ref.at[k] for k in range(4)]
    rows, orbitals = blocks[0].shape[1:]
    depth = vectors * TILE
    lane = lax.broadcasted_iota(jnp.int32, (ROW, depth), 0)
    vector = lax.shift_right_logical(lax.broadcasted_iota(jnp.int32, (ROW, depth), 1), 4)
    same = (
        jnp.bitwise_and(lax.broadcasted_iota(jnp.int32, (TILE * TILE, depth), 0), TILE - 1)
        == jnp.bitwise_and(lax.broadcasted_iota(jnp.int32, (TILE * TILE, depth), 1), TILE - 1)
    )
    weights = []
    for b in range(8):
        shifted = message_ref[place_ref[b % 4], 0:TILE, :].astype(f32)
        shifted = pltpu.roll(shifted, place_ref[4], 0).astype(bf16)
        spread = (lane == vector + TILE * (b // 4)).astype(bf16)
        wide = jnp.dot(shifted, spread, preferred_element_type=f32)
        wide = jnp.broadcast_to(wide[:, None, :], (TILE, TILE, depth)).reshape(TILE * TILE, depth)
        weights.append(jnp.where(same, wide, 0.0).astype(bf16))
    for out_ref in outs:
        out_ref[:, :, 256:WIDE] = jnp.zeros((4, rows, WIDE - 256), bf16)
    for t in range(rows // TILE):
        here = slice(t * TILE, (t + 1) * TILE)
        total = jnp.zeros((TILE * TILE, orbitals), f32)
        for b, block_ref in enumerate(blocks):
            block = block_ref[:, here, :].reshape(depth, orbitals)
            total = total + jnp.dot(weights[b], block, preferred_element_type=f32)
        total = (step_root * total).astype(bf16).reshape(TILE, TILE, orbitals)
        for w in range(TILE):
            outs[w // 4][w % 4, here, 0:orbitals] = total[w]


def field_rows(place, message, blocks, pieces):
    vectors, rows, _ = blocks[0].shape[-3:]
    return pl.pallas_call(
        functools.partial(field_kernel, vectors),
        out_shape=[jax.ShapeDtypeStruct((4 // pieces, 4, rows, WIDE), bf16)] * pieces,
        in_specs=[pl.BlockSpec(memory_space=pltpu.SMEM)]
        + [pl.BlockSpec(memory_space=pltpu.VMEM)] * (1 + len(blocks)),
        compiler_params=pltpu.CompilerParams(vmem_limit_bytes=20 * 2**20),
        cost_estimate=pl.CostEstimate(
            flops=rows * 256 * 384 * 256, bytes_accessed=rows * 40000, transcendentals=0
        ),
        name="field_rows",
    )(place, message, *blocks)


def sum_kernel(copies, message_ref, *refs):
    upper = lax.broadcasted_iota(jnp.int32, (TILE, 128), 1) >= 64
    scalars = message_ref[0, 0:TILE].astype(f32)
    for s in range(1, message_ref.shape[0]):
        scalars = scalars + message_ref[s, 0:TILE].astype(f32)
    scalars = parts_of(jnp.sum(scalars, axis=0, keepdims=True))
    out_ref = refs[-1]
    pieces = [ref.at[i] for ref in refs[:-1] for i in range(ref.shape[0])]
    firsts, seconds = pieces[:4], pieces[4:]
    groups, rows = firsts[0].shape[:2]
    for g in range(groups):
        total = firsts[0][g].astype(f32)
        below = seconds[0][g].astype(f32)
        for s in range(1, 4):
            total = total + firsts[s][g].astype(f32)
            below = below + seconds[s][g].astype(f32)
        corner = jnp.where(upper, scalars, total[0:TILE, 256:WIDE]).astype(bf16)
        total, below = total.astype(bf16), below.astype(bf16)
        for k in range(g, copies, groups):
            out_ref[k, 0:rows] = total
            out_ref[k, rows:] = below
            out_ref[k, 0:TILE, 256:WIDE] = corner


def sum_second_axis(message, first, second):
    rows, wide = first[0].shape[2] + second[0].shape[2], first[0].shape[3]
    return pl.pallas_call(
        functools.partial(sum_kernel, 8),
        out_shape=jax.ShapeDtypeStruct((8, rows, wide), bf16),
        compiler_params=pltpu.CompilerParams(vmem_limit_bytes=16 * 2**20),
        name="sum_plane",
    )(message, *first, *second)


def last_kernel(in_ref, out_ref, scalars_ref):
    total = in_ref[0].astype(f32)
    for s in range(1, in_ref.shape[0]):
        total = total + in_ref[s].astype(f32)
    rounded = total.astype(bf16)
    scalars_ref[...] = jnp.sum(total[0:TILE, 256:WIDE], axis=0, keepdims=True)
    for k in range(out_ref.shape[0]):
        out_ref[k] = rounded


def sum_over_z(received):
    _, rows, wide = received.shape
    return pl.pallas_call(
        last_kernel,
        out_shape=(
            jax.ShapeDtypeStruct((16, rows, wide), bf16),
            jax.ShapeDtypeStruct((1, 128), f32),
        ),
        compiler_params=pltpu.CompilerParams(vmem_limit_bytes=16 * 2**20),
        name="sum_z",
    )(received)


def taylor_kernel(first_rows, in_ref, walkers_ref, out_ref):
    orbitals = walkers_ref.shape[1]
    for w in range(4):
        field = jnp.concatenate(
            [in_ref[4 * k + w, 0:first_rows] for k in range(4)]
            + [in_ref[4 * w + k, first_rows:] for k in range(4)]
        )[:, 0:orbitals]
        current = walkers_ref[w]
        total = current.astype(f32)
        for order in range(1, ORDER + 1):
            update = jnp.dot(field, current, preferred_element_type=f32) / order
            total = total + update
            current = update.astype(bf16)
        out_ref[w] = total.astype(bf16)


def taylor(gathered, walkers, first_rows):
    return pl.pallas_call(
        functools.partial(taylor_kernel, first_rows),
        out_shape=jax.ShapeDtypeStruct(walkers.shape, bf16),
        compiler_params=pltpu.CompilerParams(vmem_limit_bytes=16 * 2**20),
        name="taylor",
    )(gathered, walkers)


def on_device(green, walkers, chol_rot, chol_full, fields, one_body_rot):
    x, zh, y, zl, core = (lax.axis_index(a) for a in AXES)
    vectors, electrons, orbitals = chol_rot.shape
    vector_total = vectors * 256
    group = green.shape[0]
    tiles = orbitals // TILE
    first_rows = TILE * (tiles // 8)
    second_rows = orbitals // 4 - first_rows

    def swap(a):
        return lax.ppermute(a, "core", ring(2, 1))

    turned = green.swapaxes(1, 2)
    before = lax.ppermute(turned, Z, ring(8, 1))
    behind = lax.ppermute(turned, Z, ring(8, -1))
    opposite = [(2 * i + c, 2 * ((i + 2 - 4 * c) % 8) + c) for i in range(8) for c in range(2)]
    far = lax.ppermute(turned, Z + ("core",), opposite)

    beside = swap(turned)

    first_pieces = [
        lax.dynamic_slice_in_dim(chol_full, lax.rem(x + k, 4) * first_rows, first_rows, axis=1)
        for k in range(4)
    ]
    second_piece = chol_full[:, 4 * first_rows :].reshape(vectors, 4, second_rows, orbitals)
    second_piece = second_piece.transpose(1, 0, 2, 3)

    rot = after(chol_rot.swapaxes(1, 2), *first_pieces, second_piece)
    own = pair_sums(rot, [turned, beside], True)
    arrived = lax.optimization_barrier((before, far, behind, own[0]))[:3]
    first_blocks = first_pieces[:1] + [
        lax.ppermute(after(first_pieces[k], beside), "x", ring(4, k)) for k in (1, 2, 3)
    ]
    second_block = lax.all_to_all(after(second_piece, *arrived), "y", 0, 0)

    greens = []
    for shard in arrived:
        greens += [shard, swap(shard)]
    sums = [own, pair_sums(own[2], greens, False)]

    share = walkers.shape[1]
    near = walkers.transpose(1, 0, 2).reshape(share * group, electrons)
    near = jnp.pad(near, ((0, -share * group % TILE), (0, 128 - electrons)))
    other = lax.ppermute(after(near, own[0]), "zh", ring(2, 1))
    give, keep = messages(
        jnp.stack([zl, core]).astype(jnp.int32), sums, after(fields, other, *first_blocks), turned, one_body_rot.T
    )
    got = swap(give)
    message = copies(jnp.stack([zh]).astype(jnp.int32), keep, got, near, other)
    message = after(message, second_block)
    message = lax.all_to_all(message, ("x", "y"), 0, 0)

    first_blocks = first_blocks + [swap(after(block, got)) for block in first_blocks]
    second_blocks = [second_block, swap(after(second_block, got))]

    def place(positions, shift):
        return jnp.stack([*positions, shift]).astype(jnp.int32)

    along_x = [4 * lax.rem(x + 4 - k, 4) + y for k in range(4)]
    along_y = [4 * x + k for k in range(4)]
    turn = lax.rem(16 - 4 * x, 16)
    (first,) = field_rows(place(along_x, 0), message, first_blocks, 1)
    first = lax.all_to_all(first, "y", 0, 0)
    second = field_rows(place(along_y, turn), message, second_blocks, 4)
    second = [second[0]] + [lax.ppermute(second[k], "x", ring(4, k)) for k in (1, 2, 3)]
    field = sum_second_axis(message, [first], second)
    field = lax.all_to_all(field, Z, 0, 0)
    whole = message[:, TILE:].reshape(4, 4, 2, near.shape[0], 128)[:, :, :, : share * group, :electrons]
    whole = whole.reshape(4, 4, 2, share, group, electrons).transpose(4, 0, 2, 1, 3, 5)
    whole = whole.reshape(group, orbitals, electrons)
    field, scalars = sum_over_z(field)
    scalars = scalars + swap(scalars)
    field = lax.all_to_all(field, ("x", "y"), 0, 0)
    new = taylor(field, whole, first_rows)
    new = lax.dynamic_slice_in_dim(new, share * (8 * x + 4 * zh + y), share, axis=1)
    return new, scalars[0, 64:96], scalars[0, 96:128]


def solution(mesh):
    split = Mesh(mesh.devices.reshape(SIZES), AXES)
    in_specs = (
        P(LOW, None, None),
        P(LOW, HIGH, None),
        P(HIGH + LOW, None, None),
        P(HIGH + LOW, None, None),
        P(HIGH + LOW, None),
        P(),
    )
    out_specs = (P(LOW, HIGH, None), P(), P())
    return jax.shard_map(
        on_device, mesh=split, in_specs=in_specs, out_specs=out_specs, check_vma=False
    )
```

```python
import functools

import jax
import jax.numpy as jnp
from jax import lax
from jax.experimental import pallas as pl
from jax.experimental.pallas import tpu as pltpu
from jax.sharding import Mesh, PartitionSpec as P

ORDER = 4
step_root = 0.1

AXES = ("x", "zh", "y", "zl", "core")
SIZES = (4, 2, 4, 4, 2)
Z = ("zh", "zl")
HIGH = ("x", "zh", "y")
LOW = ("zl", "core")

ROW = 128
WIDE = 384
TILE = 16
f32 = jnp.float32
bf16 = jnp.bfloat16
CONTRACT_LAST = (((1,), (1,)), ((), ()))


def after(value, *others):
    return lax.optimization_barrier((value, *others))[0]


def ring(count, shift):
    return [(i, (i + shift) % count) for i in range(count)]


def parts_of(value):
    high = value.astype(bf16).astype(f32)
    rest = value - high
    middle = rest.astype(bf16).astype(f32)
    low = (rest - middle).astype(bf16).astype(f32)
    row = lax.broadcasted_iota(jnp.int32, (TILE, value.shape[1]), 0)
    zero = jnp.zeros((TILE, value.shape[1]), f32)
    return jnp.where(
        row == 0, high, jnp.where(row == 1, middle, jnp.where(row == 2, low, zero))
    )


def pair_kernel(vectors, first, count, *refs):
    inputs, (trace_ref, square_ref) = refs[:count], refs[count : count + 2]
    rot_ref, green_ref, semaphores = refs[-3:]
    group = green_ref.shape[1]
    held = [rot_ref] + [green_ref.at[k] for k in range(count - 1)]
    loads = [
        pltpu.make_async_copy(src, dst, semaphores.at[i])
        for i, (src, dst) in enumerate(zip(inputs, held, strict=True))
    ]
    for load in loads:
        load.start()
    loads[0].wait()
    if first:
        raw_ref, rot_ref = rot_ref, refs[count + 2]
        for g in range(vectors):
            rot_ref[g] = widen(raw_ref[g]).T
    orbitals = rot_ref.shape[2]
    eye = (
        lax.broadcasted_iota(jnp.int32, (ROW, ROW), 0)
        == lax.broadcasted_iota(jnp.int32, (ROW, ROW), 1)
    ).astype(f32)

    for load in loads[1:]:
        load.wait()
    for k in range(count - 1):
        green = jnp.concatenate([widen(green_ref[k, w]) for w in range(group)], axis=1)
        rot = rot_ref[...].reshape(vectors * ROW, orbitals)
        pairs = jnp.dot(rot, green, preferred_element_type=f32)
        for w in range(group):
            total = jnp.zeros((8, ROW), f32)
            for g in range(vectors):
                block = pairs[g * ROW : (g + 1) * ROW, w * ROW : (w + 1) * ROW]
                total = total + jnp.sum((block * block.T).reshape(ROW // 8, 8, ROW), axis=0)
                trace_ref[group * k + w, pl.ds(g, 1), :] = jnp.sum(block * eye, axis=0, keepdims=True)
            square_ref[group * k + w] = total


def widen(a):
    return jnp.concatenate([a, jnp.zeros((a.shape[0], ROW - a.shape[1]), a.dtype)], axis=1)


def pair_sums(rot, greens, first):
    vectors = rot.shape[0]
    walkers = sum(g.shape[0] for g in greens)
    out_shape = [
        jax.ShapeDtypeStruct((walkers, vectors, ROW), f32),
        jax.ShapeDtypeStruct((walkers, 8, ROW), f32),
    ]
    if first:
        out_shape.append(jax.ShapeDtypeStruct((vectors, ROW, rot.shape[1]), bf16))
    return pl.pallas_call(
        functools.partial(pair_kernel, vectors, first, 1 + len(greens)),
        out_shape=out_shape,
        in_specs=[pl.BlockSpec(memory_space=pl.ANY)] * (1 + len(greens)),
        scratch_shapes=[
            pltpu.VMEM(rot.shape, bf16),
            pltpu.VMEM((len(greens), *greens[0].shape), bf16),
            pltpu.SemaphoreType.DMA((1 + len(greens),)),
        ],
        compiler_params=pltpu.CompilerParams(vmem_limit_bytes=56 * 2**20),
        cost_estimate=pl.CostEstimate(flops=1, bytes_accessed=1, transcendentals=0),
        name="pairs",
    )(rot, *greens)


def message_kernel(vector_total, place_ref, *refs):
    fields_ref, green_ref, one_body_ref, give_ref, keep_ref = refs[4:]
    traces, squares = ([ref.at[w] for ref in refs[k : k + 2] for w in range(ref.shape[0])] for k in (0, 2))
    zl, core = place_ref[0], place_ref[1]
    vectors = fields_ref.shape[0]
    lanes = lax.broadcasted_iota(jnp.int32, (vectors, 128), 1)
    lane = lax.broadcasted_iota(jnp.int32, (1, 128), 1)
    intersection = jnp.zeros((vectors, 128), f32)
    exchange = jnp.zeros((1, 128), f32)
    single = jnp.zeros((1, 128), f32)
    one_body = one_body_ref[...].astype(f32)
    for d in range(4):
        for w in range(8):
            owner = core if w < 4 else 1 - core
            index = lax.rem(zl + 4 - d, 4) * 8 + owner * 4 + w % 4
            trace = jnp.sum(traces[8 * d + w][...], axis=1, keepdims=True)
            intersection = jnp.where(lanes == index, trace, intersection)
            exchange = jnp.where(lane == index, jnp.sum(squares[8 * d + w][...], keepdims=True), exchange)
            if d == 0 and w < 4:
                own = jnp.sum(green_ref[w].astype(f32) * one_body, keepdims=True)
                single = jnp.where(lane == index, own * (2.0 / 32.0), single)
    bias = 2.0 * step_root * intersection
    noise = jnp.concatenate([fields_ref[...], jnp.zeros((vectors, 96), f32)], axis=1)
    weight = jnp.sum(noise * bias - 0.5 * bias * bias, axis=0, keepdims=True) / vector_total**0.5
    energy = jnp.sum(2.0 * intersection * intersection, axis=0, keepdims=True) - exchange
    energy = energy / vector_total + single
    shifted = jnp.concatenate([noise - bias, jnp.zeros((128 - vectors, 128), f32)]).T.astype(bf16)
    row = lax.broadcasted_iota(jnp.int32, (TILE, 128), 0)
    column = lax.broadcasted_iota(jnp.int32, (TILE, 128), 1)

    def rows_of(owner):
        source = jnp.bitwise_and(row, 3) * 8 + owner * 4 + lax.shift_right_logical(row, 2)
        return jnp.dot((column == source).astype(bf16), shifted, preferred_element_type=f32)

    scalars = parts_of(pltpu.roll(energy, 64, 1) + pltpu.roll(weight, 96, 1))
    give_ref[...] = rows_of(1 - core).astype(bf16)
    keep_ref[...] = (rows_of(core) + scalars).astype(bf16)


def messages(place, sums, fields, green, one_body):
    vectors = fields.shape[0]
    return pl.pallas_call(
        functools.partial(message_kernel, vectors * 256),
        out_shape=[jax.ShapeDtypeStruct((TILE, 128), bf16)] * 2,
        in_specs=[pl.BlockSpec(memory_space=pltpu.SMEM)]
        + [pl.BlockSpec(memory_space=pltpu.VMEM)] * 7,
        compiler_params=pltpu.CompilerParams(vmem_limit_bytes=56 * 2**20),
        name="message",
    )(place, *[p[0] for p in sums], *[p[1] for p in sums], fields, green, one_body)


def copies_kernel(place_ref, keep_ref, got_ref, near_ref, other_ref, out_ref):
    rows = near_ref.shape[0]
    near = pl.ds(pl.multiple_of(TILE + rows * place_ref[0], TILE), rows)
    other = pl.ds(pl.multiple_of(TILE + rows * (1 - place_ref[0]), TILE), rows)
    got = pltpu.roll(got_ref[...].astype(f32), TILE, 1)
    top = (keep_ref[...].astype(f32) + got).astype(bf16)
    for k in range(out_ref.shape[0]):
        out_ref[k, 0:TILE] = top
        out_ref[k, near] = near_ref[...]
        out_ref[k, other] = other_ref[...]


def copies(place, keep, got, near, other):
    return pl.pallas_call(
        copies_kernel,
        out_shape=jax.ShapeDtypeStruct((16, TILE + 2 * near.shape[0], 128), bf16),
        in_specs=[pl.BlockSpec(memory_space=pltpu.SMEM)]
        + [pl.BlockSpec(memory_space=pltpu.VMEM)] * 4,
        compiler_params=pltpu.CompilerParams(vmem_limit_bytes=16 * 2**20),
        name="copies",
    )(place, keep, got, near, other)


def field_kernel(vectors, place_ref, message_ref, *refs):
    inputs = [ref for ref in refs if len(ref.shape) == 3 or ref.shape[1] == vectors]
    outs = [out.at[i] for out in refs[len(inputs) :] for i in range(out.shape[0])]
    blocks = []
    for ref in inputs:
        blocks += [ref] if len(ref.shape) == 3 else [ref.at[k] for k in range(4)]
    rows, orbitals = blocks[0].shape[1:]
    depth = TILE * TILE
    place = lax.broadcasted_iota(jnp.int32, (ROW, 2 * depth), 1)
    spread = lax.broadcasted_iota(jnp.int32, (ROW, 2 * depth), 0) == lax.shift_right_logical(place, 4)
    spread = spread.astype(bf16)
    shifted = [
        pltpu.roll(message_ref[place_ref[k], 0:TILE, :].astype(f32), place_ref[4], 0) for k in range(4)
    ]
    shifted = jnp.concatenate(shifted).astype(bf16)
    wide = jnp.dot(shifted, spread, preferred_element_type=f32)
    same = (
        jnp.bitwise_and(lax.broadcasted_iota(jnp.int32, (depth, depth), 0), TILE - 1)
        == jnp.bitwise_and(lax.broadcasted_iota(jnp.int32, (depth, depth), 1), TILE - 1)
    )
    weights = []
    for b in range(8):
        part = wide[(b % 4) * TILE : (b % 4 + 1) * TILE, (b // 4) * depth : (b // 4 + 1) * depth]
        part = jnp.broadcast_to(part[:, None, :], (TILE, TILE, depth)).reshape(depth, depth)
        weights.append(jnp.where(same, part, 0.0).astype(bf16))
    weights = jnp.concatenate(weights, axis=1)
    nought = jnp.zeros((TILE, orbitals), bf16)
    for out_ref in outs:
        out_ref[:, :, 256:WIDE] = jnp.zeros((4, rows, WIDE - 256), bf16)
    for t in range(rows // TILE):
        here = slice(t * TILE, (t + 1) * TILE)
        column = []
        for block_ref in blocks:
            column += [block_ref[:, here, :].reshape(vectors * TILE, orbitals), nought]
        total = jnp.dot(weights, jnp.concatenate(column), preferred_element_type=f32)
        total = (step_root * total).astype(bf16).reshape(TILE, TILE, orbitals)
        for w in range(TILE):
            outs[w // 4][w % 4, here, 0:orbitals] = total[w]


def field_rows(place, message, blocks, pieces):
    vectors, rows, _ = blocks[0].shape[-3:]
    return pl.pallas_call(
        functools.partial(field_kernel, vectors),
        out_shape=[jax.ShapeDtypeStruct((4 // pieces, 4, rows, WIDE), bf16)] * pieces,
        in_specs=[pl.BlockSpec(memory_space=pltpu.SMEM)]
        + [pl.BlockSpec(memory_space=pltpu.VMEM)] * (1 + len(blocks)),
        compiler_params=pltpu.CompilerParams(vmem_limit_bytes=20 * 2**20),
        cost_estimate=pl.CostEstimate(
            flops=rows * 256 * 384 * 256, bytes_accessed=rows * 40000, transcendentals=0
        ),
        name="field_rows",
    )(place, message, *blocks)


def sum_kernel(copies, message_ref, *refs):
    upper = lax.broadcasted_iota(jnp.int32, (TILE, 128), 1) >= 64
    scalars = message_ref[0, 0:TILE].astype(f32)
    for s in range(1, message_ref.shape[0]):
        scalars = scalars + message_ref[s, 0:TILE].astype(f32)
    scalars = parts_of(jnp.sum(scalars, axis=0, keepdims=True))
    out_ref = refs[-1]
    pieces = [ref.at[i] for ref in refs[:-1] for i in range(ref.shape[0])]
    firsts, seconds = pieces[:4], pieces[4:]
    groups, rows = firsts[0].shape[:2]
    for g in range(groups):
        total = firsts[0][g].astype(f32)
        below = seconds[0][g].astype(f32)
        for s in range(1, 4):
            total = total + firsts[s][g].astype(f32)
            below = below + seconds[s][g].astype(f32)
        corner = jnp.where(upper, scalars, total[0:TILE, 256:WIDE]).astype(bf16)
        total, below = total.astype(bf16), below.astype(bf16)
        for k in range(g, copies, groups):
            out_ref[k, 0:rows] = total
            out_ref[k, rows:] = below
            out_ref[k, 0:TILE, 256:WIDE] = corner


def sum_second_axis(message, first, second):
    rows, wide = first[0].shape[2] + second[0].shape[2], first[0].shape[3]
    return pl.pallas_call(
        functools.partial(sum_kernel, 8),
        out_shape=jax.ShapeDtypeStruct((8, rows, wide), bf16),
        compiler_params=pltpu.CompilerParams(vmem_limit_bytes=16 * 2**20),
        name="sum_plane",
    )(message, *first, *second)


def last_kernel(in_ref, out_ref, scalars_ref):
    total = in_ref[0].astype(f32)
    for s in range(1, in_ref.shape[0]):
        total = total + in_ref[s].astype(f32)
    rounded = total.astype(bf16)
    scalars_ref[...] = jnp.sum(total[0:TILE, 256:WIDE], axis=0, keepdims=True)
    for k in range(out_ref.shape[0]):
        out_ref[k] = rounded


def sum_over_z(received):
    _, rows, wide = received.shape
    return pl.pallas_call(
        last_kernel,
        out_shape=(
            jax.ShapeDtypeStruct((16, rows, wide), bf16),
            jax.ShapeDtypeStruct((1, 128), f32),
        ),
        compiler_params=pltpu.CompilerParams(vmem_limit_bytes=16 * 2**20),
        name="sum_z",
    )(received)


def taylor_kernel(first_rows, in_ref, walkers_ref, out_ref):
    orbitals = walkers_ref.shape[1]
    fields = [
        jnp.concatenate(
            [in_ref[4 * k + w, 0:first_rows] for k in range(4)]
            + [in_ref[4 * w + k, first_rows:] for k in range(4)]
        )[:, 0:orbitals]
        for w in range(4)
    ]
    currents = [walkers_ref[w] for w in range(4)]
    totals = [current.astype(f32) for current in currents]
    for order in range(1, ORDER + 1):
        for w in range(4):
            update = jnp.dot(fields[w], currents[w], preferred_element_type=f32) / order
            totals[w] = totals[w] + update
            currents[w] = update.astype(bf16)
    for w in range(4):
        out_ref[w] = totals[w].astype(bf16)


def taylor(gathered, walkers, first_rows):
    return pl.pallas_call(
        functools.partial(taylor_kernel, first_rows),
        out_shape=jax.ShapeDtypeStruct(walkers.shape, bf16),
        compiler_params=pltpu.CompilerParams(vmem_limit_bytes=16 * 2**20),
        name="taylor",
    )(gathered, walkers)


def on_device(green, walkers, chol_rot, chol_full, fields, one_body_rot):
    x, zh, y, zl, core = (lax.axis_index(a) for a in AXES)
    vectors, electrons, orbitals = chol_rot.shape
    vector_total = vectors * 256
    group = green.shape[0]
    tiles = orbitals // TILE
    first_rows = TILE * (tiles // 8)
    second_rows = orbitals // 4 - first_rows

    def swap(a):
        return lax.ppermute(a, "core", ring(2, 1))

    turned = green.swapaxes(1, 2)
    before = lax.ppermute(turned, Z, ring(8, 1))
    behind = lax.ppermute(turned, Z, ring(8, -1))
    opposite = [(2 * i + c, 2 * ((i + 2 - 4 * c) % 8) + c) for i in range(8) for c in range(2)]
    far = lax.ppermute(turned, Z + ("core",), opposite)

    beside = swap(turned)

    first_pieces = [
        lax.dynamic_slice_in_dim(chol_full, lax.rem(x + k, 4) * first_rows, first_rows, axis=1)
        for k in range(4)
    ]
    second_piece = chol_full[:, 4 * first_rows :].reshape(vectors, 4, second_rows, orbitals)
    second_piece = second_piece.transpose(1, 0, 2, 3)

    rot = after(chol_rot.swapaxes(1, 2), *first_pieces, second_piece)
    own = pair_sums(rot, [turned, beside], True)
    arrived = lax.optimization_barrier((before, far, behind, own[0]))[:3]
    first_blocks = first_pieces[:1] + [
        lax.ppermute(after(first_pieces[k], beside), "x", ring(4, k)) for k in (1, 2, 3)
    ]
    second_block = lax.all_to_all(after(second_piece, *arrived), "y", 0, 0)

    greens = []
    for shard in arrived:
        greens += [shard, swap(shard)]
    sums = [own, pair_sums(own[2], greens, False)]

    share = walkers.shape[1]
    near = walkers.transpose(1, 0, 2).reshape(share * group, electrons)
    near = jnp.pad(near, ((0, -share * group % TILE), (0, 128 - electrons)))
    other = lax.ppermute(after(near, own[0]), "zh", ring(2, 1))
    give, keep = messages(
        jnp.stack([zl, core]).astype(jnp.int32), sums, after(fields, other, *first_blocks), turned, one_body_rot.T
    )
    got = swap(give)
    message = copies(jnp.stack([zh]).astype(jnp.int32), keep, got, near, other)
    message = after(message, second_block)
    message = lax.all_to_all(message, ("x", "y"), 0, 0)

    first_blocks = first_blocks + [swap(after(block, got)) for block in first_blocks]
    second_blocks = [second_block, swap(after(second_block, got))]

    def place(positions, shift):
        return jnp.stack([*positions, shift]).astype(jnp.int32)

    along_x = [4 * lax.rem(x + 4 - k, 4) + y for k in range(4)]
    along_y = [4 * x + k for k in range(4)]
    second = field_rows(place(along_y, lax.rem(16 - 4 * x, 16)), message, second_blocks, 4)
    second = [second[0]] + [lax.ppermute(second[k], "x", ring(4, k)) for k in (1, 2, 3)]
    first = field_rows(place(along_x, lax.rem(16 - 4 * y, 16)), message, first_blocks, 4)
    first = [first[0]] + [lax.ppermute(first[k], "y", ring(4, k)) for k in (1, 2, 3)]
    field = sum_second_axis(message, first, second)
    field = lax.all_to_all(field, Z, 0, 0)
    whole = message[:, TILE:].reshape(4, 4, 2, near.shape[0], 128)[:, :, :, : share * group, :electrons]
    whole = whole.reshape(4, 4, 2, share, group, electrons).transpose(4, 0, 2, 1, 3, 5)
    whole = whole.reshape(group, orbitals, electrons)
    field, scalars = sum_over_z(field)
    scalars = scalars + swap(scalars)
    field = lax.all_to_all(field, ("x", "y"), 0, 0)
    new = taylor(field, whole, first_rows)
    new = lax.dynamic_slice_in_dim(new, share * (8 * x + 4 * zh + y), share, axis=1)
    return new, scalars[0, 64:96], scalars[0, 96:128]


def solution(mesh):
    split = Mesh(mesh.devices.reshape(SIZES), AXES)
    in_specs = (
        P(LOW, None, None),
        P(LOW, HIGH, None),
        P(HIGH + LOW, None, None),
        P(HIGH + LOW, None, None),
        P(HIGH + LOW, None),
        P(),
    )
    out_specs = (P(LOW, HIGH, None), P(), P())
    return jax.shard_map(
        on_device, mesh=split, in_specs=in_specs, out_specs=out_specs, check_vma=False
    )
```

```python
import functools

import jax
import jax.numpy as jnp
from jax import lax
from jax.experimental import pallas as pl
from jax.experimental.pallas import tpu as pltpu
from jax.sharding import Mesh, PartitionSpec as P

ORDER = 4
step_root = 0.1

AXES = ("x", "zh", "y", "zl", "core")
SIZES = (4, 2, 4, 4, 2)
Z = ("zh", "zl")
HIGH = ("x", "zh", "y")
LOW = ("zl", "core")

ROW = 128
WIDE = 384
TILE = 16
f32 = jnp.float32
bf16 = jnp.bfloat16
CONTRACT_LAST = (((1,), (1,)), ((), ()))


def after(value, *others):
    return lax.optimization_barrier((value, *others))[0]


def ring(count, shift):
    return [(i, (i + shift) % count) for i in range(count)]


def parts_of(value):
    high = value.astype(bf16).astype(f32)
    rest = value - high
    middle = rest.astype(bf16).astype(f32)
    low = (rest - middle).astype(bf16).astype(f32)
    row = lax.broadcasted_iota(jnp.int32, (TILE, value.shape[1]), 0)
    zero = jnp.zeros((TILE, value.shape[1]), f32)
    return jnp.where(
        row == 0, high, jnp.where(row == 1, middle, jnp.where(row == 2, low, zero))
    )


def pair_kernel(vectors, first, count, *refs):
    inputs, (trace_ref, square_ref) = refs[:count], refs[count : count + 2]
    rot_ref, green_ref, semaphores = refs[-3:]
    group = green_ref.shape[1]
    held = [rot_ref] + [green_ref.at[k] for k in range(count - 1)]
    loads = [
        pltpu.make_async_copy(src, dst, semaphores.at[i])
        for i, (src, dst) in enumerate(zip(inputs, held, strict=True))
    ]
    for load in loads:
        load.start()
    loads[0].wait()
    if first:
        raw_ref, rot_ref = rot_ref, refs[count + 2]
        for g in range(vectors):
            rot_ref[g] = widen(raw_ref[g]).T
    orbitals = rot_ref.shape[2]
    eye = (
        lax.broadcasted_iota(jnp.int32, (ROW, ROW), 0)
        == lax.broadcasted_iota(jnp.int32, (ROW, ROW), 1)
    ).astype(f32)

    for load in loads[1:]:
        load.wait()
    for k in range(count - 1):
        green = jnp.concatenate([widen(green_ref[k, w]) for w in range(group)], axis=1)
        rot = rot_ref[...].reshape(vectors * ROW, orbitals)
        pairs = jnp.dot(rot, green, preferred_element_type=f32)
        for w in range(group):
            total = jnp.zeros((8, ROW), f32)
            for g in range(vectors):
                block = pairs[g * ROW : (g + 1) * ROW, w * ROW : (w + 1) * ROW]
                total = total + jnp.sum((block * block.T).reshape(ROW // 8, 8, ROW), axis=0)
                trace_ref[group * k + w, pl.ds(g, 1), :] = jnp.sum(block * eye, axis=0, keepdims=True)
            square_ref[group * k + w] = total


def widen(a):
    return jnp.concatenate([a, jnp.zeros((a.shape[0], ROW - a.shape[1]), a.dtype)], axis=1)


def pair_sums(rot, greens, first):
    vectors = rot.shape[0]
    walkers = sum(g.shape[0] for g in greens)
    out_shape = [
        jax.ShapeDtypeStruct((walkers, vectors, ROW), f32),
        jax.ShapeDtypeStruct((walkers, 8, ROW), f32),
    ]
    if first:
        out_shape.append(jax.ShapeDtypeStruct((vectors, ROW, rot.shape[1]), bf16))
    return pl.pallas_call(
        functools.partial(pair_kernel, vectors, first, 1 + len(greens)),
        out_shape=out_shape,
        in_specs=[pl.BlockSpec(memory_space=pl.ANY)] * (1 + len(greens)),
        scratch_shapes=[
            pltpu.VMEM(rot.shape, bf16),
            pltpu.VMEM((len(greens), *greens[0].shape), bf16),
            pltpu.SemaphoreType.DMA((1 + len(greens),)),
        ],
        compiler_params=pltpu.CompilerParams(vmem_limit_bytes=56 * 2**20),
        cost_estimate=pl.CostEstimate(flops=1, bytes_accessed=1, transcendentals=0),
        name="pairs",
    )(rot, *greens)


def message_kernel(vector_total, place_ref, *refs):
    fields_ref, green_ref, one_body_ref, give_ref, keep_ref = refs[4:]
    traces, squares = ([ref.at[w] for ref in refs[k : k + 2] for w in range(ref.shape[0])] for k in (0, 2))
    zl, core = place_ref[0], place_ref[1]
    vectors = fields_ref.shape[0]
    lanes = lax.broadcasted_iota(jnp.int32, (vectors, 128), 1)
    lane = lax.broadcasted_iota(jnp.int32, (1, 128), 1)
    intersection = jnp.zeros((vectors, 128), f32)
    exchange = jnp.zeros((1, 128), f32)
    single = jnp.zeros((1, 128), f32)
    one_body = one_body_ref[...].astype(f32)
    for d in range(4):
        for w in range(8):
            owner = core if w < 4 else 1 - core
            index = lax.rem(zl + 4 - d, 4) * 8 + owner * 4 + w % 4
            trace = jnp.sum(traces[8 * d + w][...], axis=1, keepdims=True)
            intersection = jnp.where(lanes == index, trace, intersection)
            exchange = jnp.where(lane == index, jnp.sum(squares[8 * d + w][...], keepdims=True), exchange)
            if d == 0 and w < 4:
                own = jnp.sum(green_ref[w].astype(f32) * one_body, keepdims=True)
                single = jnp.where(lane == index, own * (2.0 / 32.0), single)
    bias = 2.0 * step_root * intersection
    noise = jnp.concatenate([fields_ref[...], jnp.zeros((vectors, 96), f32)], axis=1)
    weight = jnp.sum(noise * bias - 0.5 * bias * bias, axis=0, keepdims=True) / vector_total**0.5
    energy = jnp.sum(2.0 * intersection * intersection, axis=0, keepdims=True) - exchange
    energy = energy / vector_total + single
    shifted = jnp.concatenate([noise - bias, jnp.zeros((128 - vectors, 128), f32)]).T.astype(bf16)
    row = lax.broadcasted_iota(jnp.int32, (TILE, 128), 0)
    column = lax.broadcasted_iota(jnp.int32, (TILE, 128), 1)

    def rows_of(owner):
        source = jnp.bitwise_and(row, 3) * 8 + owner * 4 + lax.shift_right_logical(row, 2)
        return jnp.dot((column == source).astype(bf16), shifted, preferred_element_type=f32)

    scalars = parts_of(pltpu.roll(energy, 64, 1) + pltpu.roll(weight, 96, 1))
    give_ref[...] = rows_of(1 - core).astype(bf16)
    keep_ref[...] = (rows_of(core) + scalars).astype(bf16)


def messages(place, sums, fields, green, one_body):
    vectors = fields.shape[0]
    return pl.pallas_call(
        functools.partial(message_kernel, vectors * 256),
        out_shape=[jax.ShapeDtypeStruct((TILE, 128), bf16)] * 2,
        in_specs=[pl.BlockSpec(memory_space=pltpu.SMEM)]
        + [pl.BlockSpec(memory_space=pltpu.VMEM)] * 7,
        compiler_params=pltpu.CompilerParams(vmem_limit_bytes=56 * 2**20),
        name="message",
    )(place, *[p[0] for p in sums], *[p[1] for p in sums], fields, green, one_body)


def copies_kernel(place_ref, keep_ref, got_ref, near_ref, other_ref, out_ref):
    rows = near_ref.shape[0]
    near = pl.ds(pl.multiple_of(TILE + rows * place_ref[0], TILE), rows)
    other = pl.ds(pl.multiple_of(TILE + rows * (1 - place_ref[0]), TILE), rows)
    got = pltpu.roll(got_ref[...].astype(f32), TILE, 1)
    top = (keep_ref[...].astype(f32) + got).astype(bf16)
    for k in range(out_ref.shape[0]):
        out_ref[k, 0:TILE] = top
        out_ref[k, near] = near_ref[...]
        out_ref[k, other] = other_ref[...]


def copies(place, keep, got, near, other):
    return pl.pallas_call(
        copies_kernel,
        out_shape=jax.ShapeDtypeStruct((16, TILE + 2 * near.shape[0], 128), bf16),
        in_specs=[pl.BlockSpec(memory_space=pltpu.SMEM)]
        + [pl.BlockSpec(memory_space=pltpu.VMEM)] * 4,
        compiler_params=pltpu.CompilerParams(vmem_limit_bytes=16 * 2**20),
        name="copies",
    )(place, keep, got, near, other)


def field_kernel(vectors, place_ref, message_ref, *refs):
    inputs = [ref for ref in refs if len(ref.shape) == 3 or ref.shape[1] == vectors]
    outs = [out.at[i] for out in refs[len(inputs) :] for i in range(out.shape[0])]
    blocks = []
    for ref in inputs:
        blocks += [ref] if len(ref.shape) == 3 else [ref.at[k] for k in range(4)]
    rows, orbitals = blocks[0].shape[1:]
    depth = TILE * TILE
    place = lax.broadcasted_iota(jnp.int32, (ROW, 2 * depth), 1)
    spread = lax.broadcasted_iota(jnp.int32, (ROW, 2 * depth), 0) == lax.shift_right_logical(place, 4)
    spread = spread.astype(bf16)
    shifted = [
        pltpu.roll(message_ref[place_ref[k], 0:TILE, :].astype(f32), place_ref[4], 0) for k in range(4)
    ]
    shifted = jnp.concatenate(shifted).astype(bf16)
    wide = jnp.dot(shifted, spread, preferred_element_type=f32)
    same = (
        jnp.bitwise_and(lax.broadcasted_iota(jnp.int32, (depth, depth), 0), TILE - 1)
        == jnp.bitwise_and(lax.broadcasted_iota(jnp.int32, (depth, depth), 1), TILE - 1)
    )
    weights = []
    for b in range(8):
        part = wide[(b % 4) * TILE : (b % 4 + 1) * TILE, (b // 4) * depth : (b // 4 + 1) * depth]
        part = jnp.broadcast_to(part[:, None, :], (TILE, TILE, depth)).reshape(depth, depth)
        weights.append(jnp.where(same, part, 0.0).astype(bf16))
    weights = jnp.concatenate(weights, axis=1)
    nought = jnp.zeros((TILE, orbitals), bf16)
    for out_ref in outs:
        out_ref[:, :, 256:WIDE] = jnp.zeros((4, rows, WIDE - 256), bf16)
    for t in range(rows // TILE):
        here = slice(t * TILE, (t + 1) * TILE)
        column = []
        for block_ref in blocks:
            column += [block_ref[:, here, :].reshape(vectors * TILE, orbitals), nought]
        total = jnp.dot(weights, jnp.concatenate(column), preferred_element_type=f32)
        total = (step_root * total).astype(bf16).reshape(TILE, TILE, orbitals)
        for w in range(TILE):
            outs[w // 4][w % 4, here, 0:orbitals] = total[w]


def field_rows(place, message, blocks, pieces):
    vectors, rows, _ = blocks[0].shape[-3:]
    return pl.pallas_call(
        functools.partial(field_kernel, vectors),
        out_shape=[jax.ShapeDtypeStruct((4 // pieces, 4, rows, WIDE), bf16)] * pieces,
        in_specs=[pl.BlockSpec(memory_space=pltpu.SMEM)]
        + [pl.BlockSpec(memory_space=pltpu.VMEM)] * (1 + len(blocks)),
        compiler_params=pltpu.CompilerParams(vmem_limit_bytes=20 * 2**20),
        cost_estimate=pl.CostEstimate(
            flops=rows * 256 * 384 * 256, bytes_accessed=rows * 40000, transcendentals=0
        ),
        name="field_rows",
    )(place, message, *blocks)


def sum_kernel(copies, message_ref, *refs):
    scalars = message_ref[0, 0:TILE].astype(f32)
    for s in range(1, message_ref.shape[0]):
        scalars = scalars + message_ref[s, 0:TILE].astype(f32)
    scalars = parts_of(jnp.sum(scalars, axis=0, keepdims=True))
    out_ref = refs[-1]
    pieces = [ref.at[i] for ref in refs[:-1] for i in range(ref.shape[0])]
    firsts, seconds = pieces[:4], pieces[4:]
    groups, rows = firsts[0].shape[:2]
    rest = seconds[0].shape[1]
    lower = lax.broadcasted_iota(jnp.int32, (rest, 128), 1) < 64
    for g in range(groups):
        total = firsts[0][g].astype(f32)
        below = seconds[0][g].astype(f32)
        for s in range(1, 4):
            total = total + firsts[s][g].astype(f32)
            below = below + seconds[s][g].astype(f32)
        last = jnp.concatenate([pltpu.roll(total[:, 256:WIDE], 64, 1), scalars])
        last = jnp.where(lower, below[:, 256:WIDE], last)
        packed = [total[:, 0:128], below[:, 0:128], total[:, 128:256], below[:, 128:256], last]
        packed = jnp.concatenate(packed).astype(bf16)
        for k in range(g, copies, groups):
            out_ref[k] = packed


def sum_second_axis(message, first, second):
    rows, rest = first[0].shape[2], second[0].shape[2]
    assert rows + TILE == rest
    return pl.pallas_call(
        functools.partial(sum_kernel, 8),
        out_shape=jax.ShapeDtypeStruct((8, 2 * rows + 3 * rest, 128), bf16),
        compiler_params=pltpu.CompilerParams(vmem_limit_bytes=16 * 2**20),
        name="sum_plane",
    )(message, *first, *second)


def last_kernel(in_ref, out_ref, scalars_ref):
    total = in_ref[0].astype(f32)
    for s in range(1, in_ref.shape[0]):
        total = total + in_ref[s].astype(f32)
    rounded = total.astype(bf16)
    scalars_ref[...] = jnp.sum(total[total.shape[0] - TILE :], axis=0, keepdims=True)
    for k in range(out_ref.shape[0]):
        out_ref[k] = rounded


def sum_over_z(received):
    _, rows, wide = received.shape
    return pl.pallas_call(
        last_kernel,
        out_shape=(
            jax.ShapeDtypeStruct((16, rows, wide), bf16),
            jax.ShapeDtypeStruct((1, 128), f32),
        ),
        compiler_params=pltpu.CompilerParams(vmem_limit_bytes=16 * 2**20),
        name="sum_z",
    )(received)


def taylor_kernel(rows, in_ref, walkers_ref, out_ref):
    orbitals = walkers_ref.shape[1]
    rest = orbitals // 4 - rows
    end = 2 * (rows + rest)

    def first_part(k):
        last = pltpu.roll(in_ref[k, end : end + rows].astype(f32), 64, 1).astype(bf16)
        return jnp.concatenate(
            [in_ref[k, 0:rows], in_ref[k, rows + rest : 2 * rows + rest], last], axis=1
        )

    def second_part(k):
        return jnp.concatenate(
            [in_ref[k, rows : rows + rest], in_ref[k, 2 * rows + rest : end], in_ref[k, end:]], axis=1
        )

    fields = [
        jnp.concatenate(
            [first_part(4 * k + w) for k in range(4)] + [second_part(4 * w + k) for k in range(4)]
        )[:, 0:orbitals]
        for w in range(4)
    ]
    currents = [walkers_ref[w] for w in range(4)]
    totals = [current.astype(f32) for current in currents]
    for order in range(1, ORDER + 1):
        for w in range(4):
            update = jnp.dot(fields[w], currents[w], preferred_element_type=f32) / order
            totals[w] = totals[w] + update
            currents[w] = update.astype(bf16)
    for w in range(4):
        out_ref[w] = totals[w].astype(bf16)


def taylor(gathered, walkers, first_rows):
    return pl.pallas_call(
        functools.partial(taylor_kernel, first_rows),
        out_shape=jax.ShapeDtypeStruct(walkers.shape, bf16),
        compiler_params=pltpu.CompilerParams(vmem_limit_bytes=16 * 2**20),
        name="taylor",
    )(gathered, walkers)


def on_device(green, walkers, chol_rot, chol_full, fields, one_body_rot):
    x, zh, y, zl, core = (lax.axis_index(a) for a in AXES)
    vectors, electrons, orbitals = chol_rot.shape
    vector_total = vectors * 256
    group = green.shape[0]
    tiles = orbitals // TILE
    first_rows = TILE * (tiles // 8)
    second_rows = orbitals // 4 - first_rows

    def swap(a):
        return lax.ppermute(a, "core", ring(2, 1))

    turned = green.swapaxes(1, 2)
    before = lax.ppermute(turned, Z, ring(8, 1))
    behind = lax.ppermute(turned, Z, ring(8, -1))
    opposite = [(2 * i + c, 2 * ((i + 2 - 4 * c) % 8) + c) for i in range(8) for c in range(2)]
    far = lax.ppermute(turned, Z + ("core",), opposite)

    beside = swap(turned)

    first_pieces = [
        lax.dynamic_slice_in_dim(chol_full, lax.rem(x + k, 4) * first_rows, first_rows, axis=1)
        for k in range(4)
    ]
    second_piece = chol_full[:, 4 * first_rows :].reshape(vectors, 4, second_rows, orbitals)
    second_piece = second_piece.transpose(1, 0, 2, 3)

    rot = after(chol_rot.swapaxes(1, 2), *first_pieces, second_piece)
    own = pair_sums(rot, [turned, beside], True)
    arrived = lax.optimization_barrier((before, far, behind, own[0]))[:3]
    first_blocks = first_pieces[:1] + [
        lax.ppermute(after(first_pieces[k], beside), "x", ring(4, k)) for k in (1, 2, 3)
    ]
    second_block = lax.all_to_all(after(second_piece, *arrived), "y", 0, 0)

    greens = []
    for shard in arrived:
        greens += [shard, swap(shard)]
    sums = [own, pair_sums(own[2], greens, False)]

    share = walkers.shape[1]
    near = walkers.transpose(1, 0, 2).reshape(share * group, electrons)
    near = jnp.pad(near, ((0, -share * group % TILE), (0, 128 - electrons)))
    other = lax.ppermute(after(near, own[0]), "zh", ring(2, 1))
    give, keep = messages(
        jnp.stack([zl, core]).astype(jnp.int32), sums, after(fields, other, *first_blocks), turned, one_body_rot.T
    )
    got = swap(give)
    message = copies(jnp.stack([zh]).astype(jnp.int32), keep, got, near, other)
    message = after(message, second_block)
    message = lax.all_to_all(message, ("x", "y"), 0, 0)

    first_blocks = first_blocks + [swap(after(block, got)) for block in first_blocks]
    second_blocks = [second_block, swap(after(second_block, got))]

    def place(positions, shift):
        return jnp.stack([*positions, shift]).astype(jnp.int32)

    along_x = [4 * lax.rem(x + 4 - k, 4) + y for k in range(4)]
    along_y = [4 * x + k for k in range(4)]
    second = field_rows(place(along_y, lax.rem(16 - 4 * x, 16)), message, second_blocks, 4)
    second = [second[0]] + [lax.ppermute(second[k], "x", ring(4, k)) for k in (1, 2, 3)]
    first = field_rows(place(along_x, lax.rem(16 - 4 * y, 16)), message, first_blocks, 4)
    first = [first[0]] + [lax.ppermute(first[k], "y", ring(4, k)) for k in (1, 2, 3)]
    field = sum_second_axis(message, first, second)
    field = lax.all_to_all(field, Z, 0, 0)
    whole = message[:, TILE:].reshape(4, 4, 2, near.shape[0], 128)[:, :, :, : share * group, :electrons]
    whole = whole.reshape(4, 4, 2, share, group, electrons).transpose(4, 0, 2, 1, 3, 5)
    whole = whole.reshape(group, orbitals, electrons)
    field, scalars = sum_over_z(field)
    scalars = scalars + swap(scalars)
    field = lax.all_to_all(field, ("x", "y"), 0, 0)
    new = taylor(field, whole, first_rows)
    new = lax.dynamic_slice_in_dim(new, share * (8 * x + 4 * zh + y), share, axis=1)
    return new, scalars[0, 64:96], scalars[0, 96:128]


def solution(mesh):
    split = Mesh(mesh.devices.reshape(SIZES), AXES)
    in_specs = (
        P(LOW, None, None),
        P(LOW, HIGH, None),
        P(HIGH + LOW, None, None),
        P(HIGH + LOW, None, None),
        P(HIGH + LOW, None),
        P(),
    )
    out_specs = (P(LOW, HIGH, None), P(), P())
    return jax.shard_map(
        on_device, mesh=split, in_specs=in_specs, out_specs=out_specs, check_vma=False
    )
```

```python
import functools

import jax
import jax.numpy as jnp
from jax import lax
from jax.experimental import pallas as pl
from jax.experimental.pallas import tpu as pltpu
from jax.sharding import Mesh, PartitionSpec as P

ORDER = 4
step_root = 0.1

AXES = ("x", "zh", "y", "zl", "core")
SIZES = (4, 2, 4, 4, 2)
Z = ("zh", "zl")
HIGH = ("x", "zh", "y")
LOW = ("zl", "core")

ROW = 128
WIDE = 384
TILE = 16
f32 = jnp.float32
bf16 = jnp.bfloat16
CONTRACT_LAST = (((1,), (1,)), ((), ()))


def after(value, *others):
    return lax.optimization_barrier((value, *others))[0]


def ring(count, shift):
    return [(i, (i + shift) % count) for i in range(count)]


def parts_of(value):
    high = value.astype(bf16).astype(f32)
    rest = value - high
    middle = rest.astype(bf16).astype(f32)
    low = (rest - middle).astype(bf16).astype(f32)
    row = lax.broadcasted_iota(jnp.int32, (TILE, value.shape[1]), 0)
    zero = jnp.zeros((TILE, value.shape[1]), f32)
    return jnp.where(
        row == 0, high, jnp.where(row == 1, middle, jnp.where(row == 2, low, zero))
    )


def pair_kernel(vectors, first, count, *refs):
    inputs, (trace_ref, square_ref) = refs[:count], refs[count : count + 2]
    rot_ref, green_ref, semaphores = refs[-3:]
    group = green_ref.shape[1]
    held = [rot_ref] + [green_ref.at[k] for k in range(count - 1)]
    loads = [
        pltpu.make_async_copy(src, dst, semaphores.at[i])
        for i, (src, dst) in enumerate(zip(inputs, held, strict=True))
    ]
    for load in loads:
        load.start()
    loads[0].wait()
    if first:
        raw_ref, rot_ref = rot_ref, refs[count + 2]
        for g in range(vectors):
            rot_ref[g] = widen(raw_ref[g]).T
    orbitals = rot_ref.shape[2]
    eye = (
        lax.broadcasted_iota(jnp.int32, (ROW, ROW), 0)
        == lax.broadcasted_iota(jnp.int32, (ROW, ROW), 1)
    ).astype(f32)

    for load in loads[1:]:
        load.wait()
    for k in range(count - 1):
        green = jnp.concatenate([widen(green_ref[k, w]) for w in range(group)], axis=1)
        rot = rot_ref[...].reshape(vectors * ROW, orbitals)
        pairs = jnp.dot(rot, green, preferred_element_type=f32)
        for w in range(group):
            total = jnp.zeros((8, ROW), f32)
            for g in range(vectors):
                block = pairs[g * ROW : (g + 1) * ROW, w * ROW : (w + 1) * ROW]
                total = total + jnp.sum((block * block.T).reshape(ROW // 8, 8, ROW), axis=0)
                trace_ref[group * k + w, pl.ds(g, 1), :] = jnp.sum(block * eye, axis=0, keepdims=True)
            square_ref[group * k + w] = total


def widen(a):
    return jnp.concatenate([a, jnp.zeros((a.shape[0], ROW - a.shape[1]), a.dtype)], axis=1)


def pair_sums(rot, greens, first):
    vectors = rot.shape[0]
    walkers = sum(g.shape[0] for g in greens)
    out_shape = [
        jax.ShapeDtypeStruct((walkers, vectors, ROW), f32),
        jax.ShapeDtypeStruct((walkers, 8, ROW), f32),
    ]
    if first:
        out_shape.append(jax.ShapeDtypeStruct((vectors, ROW, rot.shape[1]), bf16))
    return pl.pallas_call(
        functools.partial(pair_kernel, vectors, first, 1 + len(greens)),
        out_shape=out_shape,
        in_specs=[pl.BlockSpec(memory_space=pl.ANY)] * (1 + len(greens)),
        scratch_shapes=[
            pltpu.VMEM(rot.shape, bf16),
            pltpu.VMEM((len(greens), *greens[0].shape), bf16),
            pltpu.SemaphoreType.DMA((1 + len(greens),)),
        ],
        compiler_params=pltpu.CompilerParams(vmem_limit_bytes=56 * 2**20),
        cost_estimate=pl.CostEstimate(flops=1, bytes_accessed=1, transcendentals=0),
        name="pairs",
    )(rot, *greens)


def message_kernel(vector_total, place_ref, *refs):
    fields_ref, green_ref, one_body_ref, give_ref, keep_ref = refs[4:]
    traces, squares = ([ref.at[w] for ref in refs[k : k + 2] for w in range(ref.shape[0])] for k in (0, 2))
    zl, core = place_ref[0], place_ref[1]
    vectors = fields_ref.shape[0]
    lanes = lax.broadcasted_iota(jnp.int32, (vectors, 128), 1)
    lane = lax.broadcasted_iota(jnp.int32, (1, 128), 1)
    intersection = jnp.zeros((vectors, 128), f32)
    exchange = jnp.zeros((1, 128), f32)
    single = jnp.zeros((1, 128), f32)
    one_body = one_body_ref[...].astype(f32)
    for d in range(4):
        for w in range(8):
            owner = core if w < 4 else 1 - core
            index = lax.rem(zl + 4 - d, 4) * 8 + owner * 4 + w % 4
            trace = jnp.sum(traces[8 * d + w][...], axis=1, keepdims=True)
            intersection = jnp.where(lanes == index, trace, intersection)
            exchange = jnp.where(lane == index, jnp.sum(squares[8 * d + w][...], keepdims=True), exchange)
            if d == 0 and w < 4:
                own = jnp.sum(green_ref[w].astype(f32) * one_body, keepdims=True)
                single = jnp.where(lane == index, own * (2.0 / 32.0), single)
    bias = 2.0 * step_root * intersection
    noise = jnp.concatenate([fields_ref[...], jnp.zeros((vectors, 96), f32)], axis=1)
    weight = jnp.sum(noise * bias - 0.5 * bias * bias, axis=0, keepdims=True) / vector_total**0.5
    energy = jnp.sum(2.0 * intersection * intersection, axis=0, keepdims=True) - exchange
    energy = energy / vector_total + single
    shifted = jnp.concatenate([noise - bias, jnp.zeros((128 - vectors, 128), f32)]).T.astype(bf16)
    row = lax.broadcasted_iota(jnp.int32, (TILE, 128), 0)
    column = lax.broadcasted_iota(jnp.int32, (TILE, 128), 1)

    def rows_of(owner):
        source = jnp.bitwise_and(row, 3) * 8 + owner * 4 + lax.shift_right_logical(row, 2)
        return jnp.dot((column == source).astype(bf16), shifted, preferred_element_type=f32)

    scalars = parts_of(pltpu.roll(energy, 64, 1) + pltpu.roll(weight, 96, 1))
    give_ref[...] = rows_of(1 - core).astype(bf16)
    keep_ref[...] = (rows_of(core) + scalars).astype(bf16)


def messages(place, sums, fields, green, one_body):
    vectors = fields.shape[0]
    return pl.pallas_call(
        functools.partial(message_kernel, vectors * 256),
        out_shape=[jax.ShapeDtypeStruct((TILE, 128), bf16)] * 2,
        in_specs=[pl.BlockSpec(memory_space=pltpu.SMEM)]
        + [pl.BlockSpec(memory_space=pltpu.VMEM)] * 7,
        compiler_params=pltpu.CompilerParams(vmem_limit_bytes=56 * 2**20),
        name="message",
    )(place, *[p[0] for p in sums], *[p[1] for p in sums], fields, green, one_body)


def copies_kernel(place_ref, keep_ref, got_ref, near_ref, other_ref, out_ref):
    rows = near_ref.shape[0]
    near = pl.ds(pl.multiple_of(TILE + rows * place_ref[0], TILE), rows)
    other = pl.ds(pl.multiple_of(TILE + rows * (1 - place_ref[0]), TILE), rows)
    got = pltpu.roll(got_ref[...].astype(f32), TILE, 1)
    top = (keep_ref[...].astype(f32) + got).astype(bf16)
    for k in range(out_ref.shape[0]):
        out_ref[k, 0:TILE] = top
        out_ref[k, near] = near_ref[...]
        out_ref[k, other] = other_ref[...]


def copies(place, keep, got, near, other):
    return pl.pallas_call(
        copies_kernel,
        out_shape=jax.ShapeDtypeStruct((16, TILE + 2 * near.shape[0], 128), bf16),
        in_specs=[pl.BlockSpec(memory_space=pltpu.SMEM)]
        + [pl.BlockSpec(memory_space=pltpu.VMEM)] * 4,
        compiler_params=pltpu.CompilerParams(vmem_limit_bytes=16 * 2**20),
        name="copies",
    )(place, keep, got, near, other)


def field_kernel(vectors, place_ref, message_ref, *refs):
    inputs = [ref for ref in refs if len(ref.shape) == 3 or ref.shape[1] == vectors]
    outs = [out.at[i] for out in refs[len(inputs) :] for i in range(out.shape[0])]
    blocks = []
    for ref in inputs:
        blocks += [ref] if len(ref.shape) == 3 else [ref.at[k] for k in range(4)]
    rows, orbitals = blocks[0].shape[1:]
    depth = TILE * TILE
    place = lax.broadcasted_iota(jnp.int32, (ROW, 2 * depth), 1)
    spread = lax.broadcasted_iota(jnp.int32, (ROW, 2 * depth), 0) == lax.shift_right_logical(place, 4)
    spread = spread.astype(bf16)
    shifted = [
        pltpu.roll(message_ref[place_ref[k], 0:TILE, :].astype(f32), place_ref[4], 0) for k in range(4)
    ]
    shifted = jnp.concatenate(shifted).astype(bf16)
    wide = jnp.dot(shifted, spread, preferred_element_type=f32)
    same = (
        jnp.bitwise_and(lax.broadcasted_iota(jnp.int32, (depth, depth), 0), TILE - 1)
        == jnp.bitwise_and(lax.broadcasted_iota(jnp.int32, (depth, depth), 1), TILE - 1)
    )
    weights = []
    for b in range(8):
        part = wide[(b % 4) * TILE : (b % 4 + 1) * TILE, (b // 4) * depth : (b // 4 + 1) * depth]
        part = jnp.broadcast_to(part[:, None, :], (TILE, TILE, depth)).reshape(depth, depth)
        weights.append(jnp.where(same, part, 0.0).astype(bf16))
    weights = jnp.concatenate(weights, axis=1)
    nought = jnp.zeros((TILE, orbitals), bf16)
    for t in range(rows // TILE):
        here = slice(t * TILE, (t + 1) * TILE)
        column = []
        for block_ref in blocks:
            column += [block_ref[:, here, :].reshape(vectors * TILE, orbitals), nought]
        total = jnp.dot(weights, jnp.concatenate(column), preferred_element_type=f32)
        total = step_root * total
        last = total[:, 256:orbitals]
        if t % 2 == 0:
            packed = jnp.concatenate([last, jnp.zeros_like(last)], axis=1)
        else:
            packed = packed + jnp.concatenate([jnp.zeros_like(last), last], axis=1)
        for first, part in (
            (t * TILE, total[:, 0:128]),
            (rows + t * TILE, total[:, 128:256]),
            (2 * rows + t // 2 * TILE, packed),
        ):
            part = part.astype(bf16).reshape(TILE, TILE, 128)
            for w in range(TILE):
                outs[w // 4][w % 4, first : first + TILE, :] = part[w]


def packed_rows(rows):
    return 2 * rows + (rows // TILE + 1) // 2 * TILE


def field_rows(place, message, blocks, pieces):
    vectors, rows, _ = blocks[0].shape[-3:]
    return pl.pallas_call(
        functools.partial(field_kernel, vectors),
        out_shape=[jax.ShapeDtypeStruct((4 // pieces, 4, packed_rows(rows), 128), bf16)] * pieces,
        in_specs=[pl.BlockSpec(memory_space=pltpu.SMEM)]
        + [pl.BlockSpec(memory_space=pltpu.VMEM)] * (1 + len(blocks)),
        compiler_params=pltpu.CompilerParams(vmem_limit_bytes=20 * 2**20),
        cost_estimate=pl.CostEstimate(
            flops=rows * 256 * 384 * 256, bytes_accessed=rows * 40000, transcendentals=0
        ),
        name="field_rows",
    )(place, message, *blocks)


def sum_kernel(copies, message_ref, *refs):
    scalars = message_ref[0, 0:TILE].astype(f32)
    for s in range(1, message_ref.shape[0]):
        scalars = scalars + message_ref[s, 0:TILE].astype(f32)
    scalars = parts_of(jnp.sum(scalars, axis=0, keepdims=True))
    out_ref = refs[-1]
    pieces = [ref.at[i] for ref in refs[:-1] for i in range(ref.shape[0])]
    firsts, seconds = pieces[:4], pieces[4:]
    groups, rows = firsts[0].shape[:2]
    upper = lax.broadcasted_iota(jnp.int32, (TILE, 128), 1) >= 64
    for g in range(groups):
        total = firsts[0][g].astype(f32)
        below = seconds[0][g].astype(f32)
        for s in range(1, 4):
            total = total + firsts[s][g].astype(f32)
            below = below + seconds[s][g].astype(f32)
        end = jnp.where(upper, scalars, below[below.shape[0] - TILE :])
        packed = jnp.concatenate([total, below[: below.shape[0] - TILE], end]).astype(bf16)
        for k in range(g, copies, groups):
            out_ref[k] = packed


def sum_second_axis(message, first, second):
    rows = first[0].shape[2] + second[0].shape[2]
    return pl.pallas_call(
        functools.partial(sum_kernel, 8),
        out_shape=jax.ShapeDtypeStruct((8, rows, 128), bf16),
        compiler_params=pltpu.CompilerParams(vmem_limit_bytes=16 * 2**20),
        name="sum_plane",
    )(message, *first, *second)


def last_kernel(in_ref, out_ref, scalars_ref):
    total = in_ref[0].astype(f32)
    for s in range(1, in_ref.shape[0]):
        total = total + in_ref[s].astype(f32)
    rounded = total.astype(bf16)
    scalars_ref[...] = jnp.sum(total[total.shape[0] - TILE :], axis=0, keepdims=True)
    for k in range(out_ref.shape[0]):
        out_ref[k] = rounded


def sum_over_z(received):
    _, rows, wide = received.shape
    return pl.pallas_call(
        last_kernel,
        out_shape=(
            jax.ShapeDtypeStruct((16, rows, wide), bf16),
            jax.ShapeDtypeStruct((1, 128), f32),
        ),
        compiler_params=pltpu.CompilerParams(vmem_limit_bytes=16 * 2**20),
        name="sum_z",
    )(received)


def taylor_kernel(rows, in_ref, walkers_ref, out_ref):
    orbitals = walkers_ref.shape[1]
    rest = orbitals // 4 - rows

    def part(k, start, count):
        last = []
        for t in range(count // TILE):
            here = start + 2 * count + t // 2 * TILE
            tile = in_ref[k, here : here + TILE]
            last.append(pltpu.roll(tile.astype(f32), 64, 1).astype(bf16) if t % 2 else tile)
        left, right = in_ref[k, start : start + count], in_ref[k, start + count : start + 2 * count]
        return jnp.concatenate([left, right, jnp.concatenate(last)], axis=1)

    start = packed_rows(rows)
    fields = [
        jnp.concatenate(
            [part(4 * k + w, 0, rows) for k in range(4)]
            + [part(4 * w + k, start, rest) for k in range(4)]
        )[:, 0:orbitals]
        for w in range(4)
    ]
    currents = [walkers_ref[w] for w in range(4)]
    totals = [current.astype(f32) for current in currents]
    for order in range(1, ORDER + 1):
        for w in range(4):
            update = jnp.dot(fields[w], currents[w], preferred_element_type=f32) / order
            totals[w] = totals[w] + update
            currents[w] = update.astype(bf16)
    for w in range(4):
        out_ref[w] = totals[w].astype(bf16)


def taylor(gathered, walkers, first_rows):
    return pl.pallas_call(
        functools.partial(taylor_kernel, first_rows),
        out_shape=jax.ShapeDtypeStruct(walkers.shape, bf16),
        compiler_params=pltpu.CompilerParams(vmem_limit_bytes=16 * 2**20),
        name="taylor",
    )(gathered, walkers)


def on_device(green, walkers, chol_rot, chol_full, fields, one_body_rot):
    x, zh, y, zl, core = (lax.axis_index(a) for a in AXES)
    vectors, electrons, orbitals = chol_rot.shape
    vector_total = vectors * 256
    group = green.shape[0]
    tiles = orbitals // TILE
    first_rows = TILE * (tiles // 8)
    second_rows = orbitals // 4 - first_rows

    def swap(a):
        return lax.ppermute(a, "core", ring(2, 1))

    turned = green.swapaxes(1, 2)
    before = lax.ppermute(turned, Z, ring(8, 1))
    behind = lax.ppermute(turned, Z, ring(8, -1))
    opposite = [(2 * i + c, 2 * ((i + 2 - 4 * c) % 8) + c) for i in range(8) for c in range(2)]
    far = lax.ppermute(turned, Z + ("core",), opposite)

    beside = swap(turned)

    first_pieces = [
        lax.dynamic_slice_in_dim(chol_full, lax.rem(x + k, 4) * first_rows, first_rows, axis=1)
        for k in range(4)
    ]
    second_piece = chol_full[:, 4 * first_rows :].reshape(vectors, 4, second_rows, orbitals)
    second_piece = second_piece.transpose(1, 0, 2, 3)

    rot = after(chol_rot.swapaxes(1, 2), *first_pieces, second_piece)
    own = pair_sums(rot, [turned, beside], True)
    arrived = lax.optimization_barrier((before, far, behind, own[0]))[:3]
    first_blocks = first_pieces[:1] + [
        lax.ppermute(after(first_pieces[k], beside), "x", ring(4, k)) for k in (1, 2, 3)
    ]
    second_block = lax.all_to_all(after(second_piece, *arrived), "y", 0, 0)

    greens = []
    for shard in arrived:
        greens += [shard, swap(shard)]
    sums = [own, pair_sums(own[2], greens, False)]

    share = walkers.shape[1]
    near = walkers.transpose(1, 0, 2).reshape(share * group, electrons)
    near = jnp.pad(near, ((0, -share * group % TILE), (0, 128 - electrons)))
    other = lax.ppermute(after(near, own[0]), "zh", ring(2, 1))
    give, keep = messages(
        jnp.stack([zl, core]).astype(jnp.int32), sums, after(fields, other, *first_blocks), turned, one_body_rot.T
    )
    got = swap(give)
    message = copies(jnp.stack([zh]).astype(jnp.int32), keep, got, near, other)
    message = after(message, second_block)
    message = lax.all_to_all(message, ("x", "y"), 0, 0)

    first_blocks = first_blocks + [swap(after(block, got)) for block in first_blocks]
    second_blocks = [second_block, swap(after(second_block, got))]

    def place(positions, shift):
        return jnp.stack([*positions, shift]).astype(jnp.int32)

    along_x = [4 * lax.rem(x + 4 - k, 4) + y for k in range(4)]
    along_y = [4 * x + k for k in range(4)]
    second = field_rows(place(along_y, lax.rem(16 - 4 * x, 16)), message, second_blocks, 4)
    second = [second[0]] + [lax.ppermute(second[k], "x", ring(4, k)) for k in (1, 2, 3)]
    first = field_rows(place(along_x, lax.rem(16 - 4 * y, 16)), message, first_blocks, 4)
    first = [first[0]] + [lax.ppermute(first[k], "y", ring(4, k)) for k in (1, 2, 3)]
    field = sum_second_axis(message, first, second)
    field = lax.all_to_all(field, Z, 0, 0)
    whole = message[:, TILE:].reshape(4, 4, 2, near.shape[0], 128)[:, :, :, : share * group, :electrons]
    whole = whole.reshape(4, 4, 2, share, group, electrons).transpose(4, 0, 2, 1, 3, 5)
    whole = whole.reshape(group, orbitals, electrons)
    field, scalars = sum_over_z(field)
    scalars = scalars + swap(scalars)
    field = lax.all_to_all(field, ("x", "y"), 0, 0)
    new = taylor(field, whole, first_rows)
    new = lax.dynamic_slice_in_dim(new, share * (8 * x + 4 * zh + y), share, axis=1)
    return new, scalars[0, 64:96], scalars[0, 96:128]


def solution(mesh):
    split = Mesh(mesh.devices.reshape(SIZES), AXES)
    in_specs = (
        P(LOW, None, None),
        P(LOW, HIGH, None),
        P(HIGH + LOW, None, None),
        P(HIGH + LOW, None, None),
        P(HIGH + LOW, None),
        P(),
    )
    out_specs = (P(LOW, HIGH, None), P(), P())
    return jax.shard_map(
        on_device, mesh=split, in_specs=in_specs, out_specs=out_specs, check_vma=False
    )
```

```python
import functools

import jax
import jax.numpy as jnp
from jax import lax
from jax.experimental import pallas as pl
from jax.experimental.pallas import tpu as pltpu
from jax.sharding import Mesh, PartitionSpec as P

ORDER = 4
step_root = 0.1

AXES = ("x", "zh", "y", "zl", "core")
SIZES = (4, 2, 4, 4, 2)
Z = ("zh", "zl")
HIGH = ("x", "zh", "y")
LOW = ("zl", "core")

ROW = 128
WIDE = 384
TILE = 16
f32 = jnp.float32
bf16 = jnp.bfloat16
CONTRACT_LAST = (((1,), (1,)), ((), ()))


def after(value, *others):
    return lax.optimization_barrier((value, *others))[0]


def ring(count, shift):
    return [(i, (i + shift) % count) for i in range(count)]


def parts_of(value):
    high = value.astype(bf16).astype(f32)
    rest = value - high
    middle = rest.astype(bf16).astype(f32)
    low = (rest - middle).astype(bf16).astype(f32)
    row = lax.broadcasted_iota(jnp.int32, (TILE, value.shape[1]), 0)
    zero = jnp.zeros((TILE, value.shape[1]), f32)
    return jnp.where(
        row == 0, high, jnp.where(row == 1, middle, jnp.where(row == 2, low, zero))
    )


def pair_kernel(vectors, first, count, *refs):
    inputs, (trace_ref, square_ref) = refs[:count], refs[count : count + 2]
    rot_ref, green_ref, semaphores = refs[-3:]
    group = green_ref.shape[1]
    held = [rot_ref] + [green_ref.at[k] for k in range(count - 1)]
    loads = [
        pltpu.make_async_copy(src, dst, semaphores.at[i])
        for i, (src, dst) in enumerate(zip(inputs, held, strict=True))
    ]
    for load in loads:
        load.start()
    loads[0].wait()
    if first:
        raw_ref, rot_ref = rot_ref, refs[count + 2]
        for g in range(vectors):
            rot_ref[g] = widen(raw_ref[g]).T
    orbitals = rot_ref.shape[2]
    eye = (
        lax.broadcasted_iota(jnp.int32, (ROW, ROW), 0)
        == lax.broadcasted_iota(jnp.int32, (ROW, ROW), 1)
    ).astype(f32)

    for load in loads[1:]:
        load.wait()
    for k in range(count - 1):
        green = jnp.concatenate([widen(green_ref[k, w]) for w in range(group)], axis=1)
        rot = rot_ref[...].reshape(vectors * ROW, orbitals)
        pairs = jnp.dot(rot, green, preferred_element_type=f32)
        for w in range(group):
            total = jnp.zeros((8, ROW), f32)
            for g in range(vectors):
                block = pairs[g * ROW : (g + 1) * ROW, w * ROW : (w + 1) * ROW]
                total = total + jnp.sum((block * block.T).reshape(ROW // 8, 8, ROW), axis=0)
                trace_ref[group * k + w, pl.ds(g, 1), :] = jnp.sum(block * eye, axis=0, keepdims=True)
            square_ref[group * k + w] = total


def widen(a):
    return jnp.concatenate([a, jnp.zeros((a.shape[0], ROW - a.shape[1]), a.dtype)], axis=1)


def pair_sums(rot, greens, first):
    vectors = rot.shape[0]
    walkers = sum(g.shape[0] for g in greens)
    out_shape = [
        jax.ShapeDtypeStruct((walkers, vectors, ROW), f32),
        jax.ShapeDtypeStruct((walkers, 8, ROW), f32),
    ]
    if first:
        out_shape.append(jax.ShapeDtypeStruct((vectors, ROW, rot.shape[1]), bf16))
    return pl.pallas_call(
        functools.partial(pair_kernel, vectors, first, 1 + len(greens)),
        out_shape=out_shape,
        in_specs=[pl.BlockSpec(memory_space=pl.ANY)] * (1 + len(greens)),
        scratch_shapes=[
            pltpu.VMEM(rot.shape, bf16),
            pltpu.VMEM((len(greens), *greens[0].shape), bf16),
            pltpu.SemaphoreType.DMA((1 + len(greens),)),
        ],
        compiler_params=pltpu.CompilerParams(vmem_limit_bytes=56 * 2**20),
        cost_estimate=pl.CostEstimate(flops=1, bytes_accessed=1, transcendentals=0),
        name="pairs",
    )(rot, *greens)


def message_kernel(vector_total, place_ref, *refs):
    fields_ref, green_ref, one_body_ref, give_ref, keep_ref = refs[4:]
    traces, squares = ([ref.at[w] for ref in refs[k : k + 2] for w in range(ref.shape[0])] for k in (0, 2))
    zl, core = place_ref[0], place_ref[1]
    vectors = fields_ref.shape[0]
    lanes = lax.broadcasted_iota(jnp.int32, (vectors, 128), 1)
    lane = lax.broadcasted_iota(jnp.int32, (1, 128), 1)
    intersection = jnp.zeros((vectors, 128), f32)
    exchange = jnp.zeros((1, 128), f32)
    single = jnp.zeros((1, 128), f32)
    one_body = one_body_ref[...].astype(f32)
    for d in range(4):
        for w in range(8):
            owner = core if w < 4 else 1 - core
            index = lax.rem(zl + 4 - d, 4) * 8 + owner * 4 + w % 4
            trace = jnp.sum(traces[8 * d + w][...], axis=1, keepdims=True)
            intersection = jnp.where(lanes == index, trace, intersection)
            exchange = jnp.where(lane == index, jnp.sum(squares[8 * d + w][...], keepdims=True), exchange)
            if d == 0 and w < 4:
                own = jnp.sum(green_ref[w].astype(f32) * one_body, keepdims=True)
                single = jnp.where(lane == index, own * (2.0 / 32.0), single)
    bias = 2.0 * step_root * intersection
    noise = jnp.concatenate([fields_ref[...], jnp.zeros((vectors, 96), f32)], axis=1)
    weight = jnp.sum(noise * bias - 0.5 * bias * bias, axis=0, keepdims=True) / vector_total**0.5
    energy = jnp.sum(2.0 * intersection * intersection, axis=0, keepdims=True) - exchange
    energy = energy / vector_total + single
    shifted = jnp.concatenate([noise - bias, jnp.zeros((128 - vectors, 128), f32)]).T.astype(bf16)
    row = lax.broadcasted_iota(jnp.int32, (TILE, 128), 0)
    column = lax.broadcasted_iota(jnp.int32, (TILE, 128), 1)

    def rows_of(owner):
        source = jnp.bitwise_and(row, 3) * 8 + owner * 4 + lax.shift_right_logical(row, 2)
        return jnp.dot((column == source).astype(bf16), shifted, preferred_element_type=f32)

    scalars = parts_of(pltpu.roll(energy, 64, 1) + pltpu.roll(weight, 96, 1))
    give_ref[...] = rows_of(1 - core).astype(bf16)
    keep_ref[...] = (rows_of(core) + scalars).astype(bf16)


def messages(place, sums, fields, green, one_body):
    vectors = fields.shape[0]
    return pl.pallas_call(
        functools.partial(message_kernel, vectors * 256),
        out_shape=[jax.ShapeDtypeStruct((TILE, 128), bf16)] * 2,
        in_specs=[pl.BlockSpec(memory_space=pltpu.SMEM)]
        + [pl.BlockSpec(memory_space=pltpu.VMEM)] * 7,
        compiler_params=pltpu.CompilerParams(vmem_limit_bytes=56 * 2**20),
        name="message",
    )(place, *[p[0] for p in sums], *[p[1] for p in sums], fields, green, one_body)


def copies_kernel(place_ref, keep_ref, got_ref, near_ref, other_ref, out_ref):
    rows = near_ref.shape[0]
    near = pl.ds(pl.multiple_of(TILE + rows * place_ref[0], TILE), rows)
    other = pl.ds(pl.multiple_of(TILE + rows * (1 - place_ref[0]), TILE), rows)
    got = pltpu.roll(got_ref[...].astype(f32), TILE, 1)
    top = (keep_ref[...].astype(f32) + got).astype(bf16)
    for k in range(out_ref.shape[0]):
        out_ref[k, 0:TILE] = top
        out_ref[k, near] = near_ref[...]
        out_ref[k, other] = other_ref[...]


def copies(place, keep, got, near, other):
    return pl.pallas_call(
        copies_kernel,
        out_shape=jax.ShapeDtypeStruct((16, TILE + 2 * near.shape[0], 128), bf16),
        in_specs=[pl.BlockSpec(memory_space=pltpu.SMEM)]
        + [pl.BlockSpec(memory_space=pltpu.VMEM)] * 4,
        compiler_params=pltpu.CompilerParams(vmem_limit_bytes=16 * 2**20),
        name="copies",
    )(place, keep, got, near, other)


def field_kernel(vectors, place_ref, message_ref, *refs):
    inputs = [ref for ref in refs if len(ref.shape) == 3 or ref.shape[1] == vectors]
    outs = [out.at[i] for out in refs[len(inputs) :] for i in range(out.shape[0])]
    blocks = []
    for ref in inputs:
        blocks += [ref] if len(ref.shape) == 3 else [ref.at[k] for k in range(4)]
    rows, orbitals = blocks[0].shape[1:]
    depth = TILE * TILE
    place = lax.broadcasted_iota(jnp.int32, (ROW, 2 * depth), 1)
    spread = lax.broadcasted_iota(jnp.int32, (ROW, 2 * depth), 0) == lax.shift_right_logical(place, 4)
    spread = spread.astype(bf16)
    shifted = [
        pltpu.roll(message_ref[place_ref[k], 0:TILE, :].astype(f32), place_ref[4], 0) for k in range(4)
    ]
    shifted = jnp.concatenate(shifted).astype(bf16)
    wide = jnp.dot(shifted, spread, preferred_element_type=f32)
    same = (
        jnp.bitwise_and(lax.broadcasted_iota(jnp.int32, (depth, depth), 0), TILE - 1)
        == jnp.bitwise_and(lax.broadcasted_iota(jnp.int32, (depth, depth), 1), TILE - 1)
    )
    weights = []
    for b in range(8):
        part = wide[(b % 4) * TILE : (b % 4 + 1) * TILE, (b // 4) * depth : (b // 4 + 1) * depth]
        part = jnp.broadcast_to(part[:, None, :], (TILE, TILE, depth)).reshape(depth, depth)
        weights.append(jnp.where(same, part, 0.0).astype(bf16))
    weights = jnp.concatenate(weights, axis=1)
    nought = jnp.zeros((TILE, orbitals), bf16)
    for t in range(rows // TILE):
        here = slice(t * TILE, (t + 1) * TILE)
        column = []
        for block_ref in blocks:
            column += [block_ref[:, here, :].reshape(vectors * TILE, orbitals), nought]
        total = jnp.dot(weights, jnp.concatenate(column), preferred_element_type=f32)
        total = step_root * total
        last = total[:, 256:orbitals]
        if t % 2 == 0:
            packed = jnp.concatenate([last, jnp.zeros_like(last)], axis=1)
        else:
            packed = packed + jnp.concatenate([jnp.zeros_like(last), last], axis=1)
        for first, part in (
            (t * TILE, total[:, 0:128]),
            (rows + t * TILE, total[:, 128:256]),
            (2 * rows + t // 2 * TILE, packed),
        ):
            part = part.astype(bf16).reshape(TILE, TILE, 128)
            for w in range(TILE):
                outs[w // 4][w % 4, first : first + TILE, :] = part[w]


def packed_rows(rows):
    return 2 * rows + (rows // TILE + 1) // 2 * TILE


def field_rows(place, message, blocks, pieces):
    vectors, rows, _ = blocks[0].shape[-3:]
    return pl.pallas_call(
        functools.partial(field_kernel, vectors),
        out_shape=[jax.ShapeDtypeStruct((4 // pieces, 4, packed_rows(rows), 128), bf16)] * pieces,
        in_specs=[pl.BlockSpec(memory_space=pltpu.SMEM)]
        + [pl.BlockSpec(memory_space=pltpu.VMEM)] * (1 + len(blocks)),
        compiler_params=pltpu.CompilerParams(vmem_limit_bytes=20 * 2**20),
        cost_estimate=pl.CostEstimate(
            flops=rows * 256 * 384 * 256, bytes_accessed=rows * 40000, transcendentals=0
        ),
        name="field_rows",
    )(place, message, *blocks)


def sum_kernel(copies, message_ref, *refs):
    scalars = message_ref[0, 0:TILE].astype(f32)
    for s in range(1, message_ref.shape[0]):
        scalars = scalars + message_ref[s, 0:TILE].astype(f32)
    scalars = parts_of(jnp.sum(scalars, axis=0, keepdims=True))
    out_ref = refs[-1]
    pieces = [ref.at[i] for ref in refs[:-1] for i in range(ref.shape[0])]
    firsts, seconds = pieces[:4], pieces[4:]
    groups, rows = firsts[0].shape[:2]
    upper = lax.broadcasted_iota(jnp.int32, (TILE, 128), 1) >= 64
    for g in range(groups):
        total = firsts[0][g].astype(f32)
        below = seconds[0][g].astype(f32)
        for s in range(1, 4):
            total = total + firsts[s][g].astype(f32)
            below = below + seconds[s][g].astype(f32)
        end = jnp.where(upper, scalars, below[below.shape[0] - TILE :])
        packed = jnp.concatenate([total, below[: below.shape[0] - TILE], end]).astype(bf16)
        for k in range(g, copies, groups):
            out_ref[k] = packed


def sum_second_axis(message, first, second):
    rows = first[0].shape[2] + second[0].shape[2]
    return pl.pallas_call(
        functools.partial(sum_kernel, 8),
        out_shape=jax.ShapeDtypeStruct((8, rows, 128), bf16),
        compiler_params=pltpu.CompilerParams(vmem_limit_bytes=16 * 2**20),
        name="sum_plane",
    )(message, *first, *second)


def last_kernel(in_ref, out_ref, scalars_ref):
    total = in_ref[0].astype(f32)
    for s in range(1, in_ref.shape[0]):
        total = total + in_ref[s].astype(f32)
    rounded = total.astype(bf16)
    scalars_ref[...] = jnp.sum(total[total.shape[0] - TILE :], axis=0, keepdims=True)
    for k in range(out_ref.shape[0]):
        out_ref[k] = rounded


def sum_over_z(received):
    _, rows, wide = received.shape
    return pl.pallas_call(
        last_kernel,
        out_shape=(
            jax.ShapeDtypeStruct((16, rows, wide), bf16),
            jax.ShapeDtypeStruct((1, 128), f32),
        ),
        compiler_params=pltpu.CompilerParams(vmem_limit_bytes=16 * 2**20),
        name="sum_z",
    )(received)


def taylor_kernel(rows, in_ref, walkers_ref, out_ref):
    orbitals = walkers_ref.shape[1]
    rest = orbitals // 4 - rows

    def part(k, start, count):
        last = []
        for t in range(count // TILE):
            here = start + 2 * count + t // 2 * TILE
            tile = in_ref[k, here : here + TILE]
            last.append(pltpu.roll(tile.astype(f32), 64, 1).astype(bf16) if t % 2 else tile)
        left, right = in_ref[k, start : start + count], in_ref[k, start + count : start + 2 * count]
        return jnp.concatenate([left, right, jnp.concatenate(last)], axis=1)

    start = packed_rows(rows)
    fields = [
        jnp.concatenate(
            [part(4 * k + w, 0, rows) for k in range(4)]
            + [part(4 * w + k, start, rest) for k in range(4)]
        )[:, 0:orbitals]
        for w in range(4)
    ]
    currents = [walkers_ref[w] for w in range(4)]
    totals = [current.astype(f32) for current in currents]
    for order in range(1, ORDER + 1):
        for w in range(4):
            update = jnp.dot(fields[w], currents[w], preferred_element_type=f32) / order
            totals[w] = totals[w] + update
            currents[w] = update.astype(bf16)
    for w in range(4):
        out_ref[w] = totals[w].astype(bf16)


def taylor(gathered, walkers, first_rows):
    return pl.pallas_call(
        functools.partial(taylor_kernel, first_rows),
        out_shape=jax.ShapeDtypeStruct(walkers.shape, bf16),
        compiler_params=pltpu.CompilerParams(vmem_limit_bytes=16 * 2**20),
        name="taylor",
    )(gathered, walkers)


def on_device(green, walkers, chol_rot, chol_full, fields, one_body_rot):
    x, zh, y, zl, core = (lax.axis_index(a) for a in AXES)
    vectors, electrons, orbitals = chol_rot.shape
    vector_total = vectors * 256
    group = green.shape[0]
    tiles = orbitals // TILE
    first_rows = TILE * (tiles // 8)
    second_rows = orbitals // 4 - first_rows

    def swap(a):
        return lax.ppermute(a, "core", ring(2, 1))

    turned = green.swapaxes(1, 2)
    before = lax.ppermute(turned, Z, ring(8, 1))
    behind = lax.ppermute(turned, Z, ring(8, -1))
    opposite = [(2 * i + c, 2 * ((i + 2 - 4 * c) % 8) + c) for i in range(8) for c in range(2)]
    far = lax.ppermute(turned, Z + ("core",), opposite)

    beside = swap(turned)

    first_pieces = [
        lax.dynamic_slice_in_dim(chol_full, lax.rem(x + k, 4) * first_rows, first_rows, axis=1)
        for k in range(4)
    ]
    second_piece = chol_full[:, 4 * first_rows :].reshape(vectors, 4, second_rows, orbitals)
    second_piece = second_piece.transpose(1, 0, 2, 3)

    rot = after(chol_rot.swapaxes(1, 2), *first_pieces, second_piece)
    own = pair_sums(rot, [turned, beside], True)
    arrived = lax.optimization_barrier((before, far, behind, own[0]))[:3]
    first_blocks = first_pieces[:1] + [
        lax.ppermute(after(first_pieces[k], beside), "x", ring(4, k)) for k in (1, 2, 3)
    ]
    second_block = lax.all_to_all(after(second_piece, *arrived), "y", 0, 0)

    greens = []
    for shard in arrived:
        greens += [shard, swap(shard)]
    sums = [own, pair_sums(own[2], greens, False)]

    share = walkers.shape[1]
    near = walkers.transpose(1, 0, 2).reshape(share * group, electrons)
    near = jnp.pad(near, ((0, -share * group % TILE), (0, 128 - electrons)))
    other = lax.ppermute(after(near, own[0]), "zh", ring(2, 1))
    give, keep = messages(
        jnp.stack([zl, core]).astype(jnp.int32), sums, after(fields, other, *first_blocks), turned, one_body_rot.T
    )
    got = swap(give)
    message = copies(jnp.stack([zh]).astype(jnp.int32), keep, got, near, other)
    message = after(message, second_block)
    message = lax.all_to_all(message, ("x", "y"), 0, 0)

    first_blocks = first_blocks + [swap(after(block, got)) for block in first_blocks]
    second_blocks = [second_block, swap(after(second_block, got))]

    def place(positions, shift):
        return jnp.stack([*positions, shift]).astype(jnp.int32)

    along_x = [4 * lax.rem(x + 4 - k, 4) + y for k in range(4)]
    along_y = [4 * x + k for k in range(4)]
    second = field_rows(place(along_y, lax.rem(16 - 4 * x, 16)), message, second_blocks, 4)
    second = [second[0]] + [lax.ppermute(second[k], "x", ring(4, k)) for k in (1, 2, 3)]
    later = after(message, second[0])
    first = field_rows(place(along_x, lax.rem(16 - 4 * y, 16)), later, first_blocks, 4)
    first = [first[0]] + [lax.ppermute(first[k], "y", ring(4, k)) for k in (1, 2, 3)]
    field = sum_second_axis(message, first, second)
    field = lax.all_to_all(field, Z, 0, 0)
    whole = message[:, TILE:].reshape(4, 4, 2, near.shape[0], 128)[:, :, :, : share * group, :electrons]
    whole = whole.reshape(4, 4, 2, share, group, electrons).transpose(4, 0, 2, 1, 3, 5)
    whole = whole.reshape(group, orbitals, electrons)
    field, scalars = sum_over_z(field)
    scalars = scalars + swap(scalars)
    field = lax.all_to_all(field, ("x", "y"), 0, 0)
    new = taylor(field, whole, first_rows)
    new = lax.dynamic_slice_in_dim(new, share * (8 * x + 4 * zh + y), share, axis=1)
    return new, scalars[0, 64:96], scalars[0, 96:128]


def solution(mesh):
    split = Mesh(mesh.devices.reshape(SIZES), AXES)
    in_specs = (
        P(LOW, None, None),
        P(LOW, HIGH, None),
        P(HIGH + LOW, None, None),
        P(HIGH + LOW, None, None),
        P(HIGH + LOW, None),
        P(),
    )
    out_specs = (P(LOW, HIGH, None), P(), P())
    return jax.shard_map(
        on_device, mesh=split, in_specs=in_specs, out_specs=out_specs, check_vma=False
    )
```
